32 devices in a mesh: scan: 2 (over y), ang: 4 (over z), row: 4 (over x, core).
Axes of the slice: x: 2, y: 2, z: 4, core: 2. Of those that a mesh axis runs over, the one named last changes fastest.
Arguments:
- raw_frames: bfloat16 [96, 128, 2560], P(('scan', 'ang'), 'row'), parts along dimension 0, may hold values from 0.099609375 to 1.5
- dark_field: bfloat16 [128, 2560], P('row'), may hold values from 0 to 0.079589844
- flat_field: bfloat16 [128, 2560], P('row'), may hold values from 0.796875 to 1.1953125
- kernel_taps: float32 [31], replicated, may hold values from 0.1 to 0.4
- partner: int32 [48], P('scan'), parts along dimension 0, may hold values from 24 to 47, as said below
- shifts: int32 [256], replicated, may hold values from -256 to 255, as said below
Outputs:
- sinograms: bfloat16 [96, 128, 2560], P('scan', ('ang', 'row')), parts along dimension 0
- correlation: float32 [256, 256], P(('scan', 'ang', 'row')), parts along dimension 0
The draws below stay inside these ranges and needn't reach their ends.
There are 2 independent parts, one for each index of `scan`. The reference program is written for one: setup_inputs(seed, part) draws one part's arguments, and reference() takes and returns one part's arrays. A program takes and returns all parts, laid end to end along the dimension named above; an argument that names none is the same for every part. Nothing has to cross between parts.
Inputs may be any that keep to these rules, and one draw needn't show every extreme that they name: partner[i] - i - 24 is -1, 0 or 1 for every i; partner[0] = 24 and partner[23] = 47. shifts[0] = -256 and shifts[255] = 255; values may repeat.
All inputs are finite; a program needn't handle non-finite values.
Results may differ from the reference program's by a relative error of at most 0.012.
The reference program's roundings to bfloat16 on the way (of `centered`, `ramp_kernel` and `mirrored`) count: a program that leaves them out, or rounds other values in their place, can miss the bound.
Values may be sent and summed in bfloat16 or wider, within the bound.
No kernel may reach another device: no remote copies, remote signals or barrier semaphores. Data moves between devices by JAX's collectives and lax.ppermute only.
A program may use at most 128 MiB of HBM per device.

```python
import math
import jax
import jax.numpy as jnp
from jax import lax

C = 2560
TAPS = 31
SPAN = 256
NSHIFT = 256
NPROJ = 48
ROWS = 128
HALF = 24


def draw_partner(key, part):
    jitter = jax.random.randint(key, (NPROJ // 2,), -1, 2)
    position = jnp.arange(NPROJ // 2, dtype=jnp.int32)
    jitter = jnp.where(position == 0, 0, jitter)
    jitter = jnp.where(position == NPROJ // 2 - 1, 0, jitter)
    return (position + NPROJ // 2 + jitter).astype(jnp.int32)


def draw_shifts(key, part):
    values = jax.random.randint(key, (NSHIFT,), -SPAN, SPAN)
    position = jnp.arange(NSHIFT, dtype=jnp.int32)
    values = jnp.where(position == 0, -SPAN, values)
    values = jnp.where(position == NSHIFT - 1, SPAN - 1, values)
    return values.astype(jnp.int32)


def block_levels(rng, shape, cuts, smallest, largest):
    loudness, own = 1.0, jax.random.fold_in(rng, 6)
    for axis_at, blocks in cuts:
        draws = jnp.exp(jax.random.uniform(jax.random.fold_in(own, axis_at), (blocks,), jnp.float32, smallest / len(cuts), largest / len(cuts)))
        loudness = loudness * jnp.repeat(draws, shape[axis_at] // blocks).reshape([-1 if axis == axis_at else 1 for axis in range(len(shape))])
    return loudness


def setup_inputs(seed: int = 0, part: int = 0) -> dict:
    arg_keys = jax.random.split(jax.random.key(seed), 7)
    part_splits = jax.random.split(jax.random.fold_in(arg_keys[6], part), 7)
    return {
        "raw_frames": jnp.clip(0.099609375 + 1.4003906 * jax.random.uniform(part_splits[0], (NPROJ, ROWS, C), jnp.float32) ** block_levels(part_splits[0], (NPROJ, ROWS, C), ((0, 4), (1, 4)), -0.2, 0.2), 0.099609375, 1.5).astype(jnp.bfloat16),
        "dark_field": jnp.clip(0.079589844 * jax.random.uniform(arg_keys[1], (ROWS, C), jnp.float32) ** block_levels(arg_keys[1], (ROWS, C), ((0, 4),), -0.2, 0.2), 0.0, 0.079589844).astype(jnp.bfloat16),
        "flat_field": jnp.clip(0.796875 + 0.3984375 * jax.random.uniform(arg_keys[2], (ROWS, C), jnp.float32) ** block_levels(arg_keys[2], (ROWS, C), ((0, 4),), -0.2, 0.2), 0.796875, 1.1953125).astype(jnp.bfloat16),
        "kernel_taps": jnp.clip(jnp.exp(jax.random.uniform(arg_keys[3], (TAPS,), jnp.float32, math.log(0.1), math.log(0.4))), 0.1, 0.4),
        "partner": draw_partner(jax.random.fold_in(jax.random.fold_in(arg_keys[6], part), 71), part),
        "shifts": draw_shifts(jax.random.fold_in(arg_keys[6], 71), part),
    }


def absorb(raw_frames, dark_field, flat_field):
    counts = raw_frames.astype(jnp.float32)
    darkness = dark_field.astype(jnp.float32)
    brightness = flat_field.astype(jnp.float32)
    return -jnp.log((counts - darkness) / (brightness - darkness))


def column_pass(signal, kernel_taps):
    margin = kernel_taps.shape[0] // 2
    col_count = signal.shape[-1]
    padding = [(0, 0)] * (signal.ndim - 1) + [(margin, margin)]
    padded = jnp.pad(signal, padding)
    summed = kernel_taps[0] * padded[..., 0:col_count]
    for tap_index in range(1, kernel_taps.shape[0]):
        summed = summed + kernel_taps[tap_index] * padded[..., tap_index:tap_index + col_count]
    return summed


def row_pass(extended, kernel_taps, row_count, row_axis):
    summed = kernel_taps[0] * lax.slice_in_dim(extended, 0, row_count, axis=row_axis)
    for tap_index in range(1, kernel_taps.shape[0]):
        summed = summed + kernel_taps[tap_index] * lax.slice_in_dim(extended, tap_index, tap_index + row_count, axis=row_axis)
    return summed


def center_lines(lowpassed):
    return (lowpassed - jnp.mean(lowpassed, axis=-1, keepdims=True)).astype(jnp.bfloat16)


def ramp_matrix(col_count):
    distance = lax.iota(jnp.int32, col_count)[:, None] - lax.iota(jnp.int32, col_count)[None, :]
    spacing = distance.astype(jnp.float32)
    odd_distance = (distance % 2) != 0
    falloff = -4.0 / (math.pi * math.pi * jnp.maximum(spacing * spacing, 1.0))
    kernel = jnp.where(distance == 0, 1.0, jnp.where(odd_distance, falloff, 0.0))
    return kernel.astype(jnp.bfloat16)


def reference(raw_frames, dark_field, flat_field, kernel_taps, partner, shifts):
    margin = TAPS // 2
    ramp_kernel = ramp_matrix(C).astype(jnp.float32)

    def one_plane(frame_in):
        smooth = column_pass(absorb(frame_in, dark_field, flat_field), kernel_taps)
        extended = jnp.pad(smooth, ((margin, margin), (0, 0)))
        lowpassed = row_pass(extended, kernel_taps, ROWS, 0)
        centered = center_lines(lowpassed)
        filtered = jnp.dot(centered.astype(jnp.float32), ramp_kernel, precision=lax.Precision.HIGHEST)
        return centered, filtered.astype(jnp.bfloat16)

    centered, sinograms = lax.map(one_plane, raw_frames)
    factor = (HALF * C) ** -0.5

    def one_row(row_index):
        column = lax.dynamic_index_in_dim(centered, row_index, 1, False)
        leading = column[:HALF].astype(jnp.float32)
        mirrored = jnp.flip(jnp.take(column, partner, axis=0), axis=1).astype(jnp.float32)
        product = jnp.dot(leading.T, mirrored, precision=lax.Precision.HIGHEST)
        padded = jnp.pad(product, ((0, 0), (SPAN, SPAN)))
        window_width = C + 2 * SPAN
        flattened = jnp.pad(padded.reshape(-1), (0, C))
        skewed = flattened.reshape(C, window_width + 1)[:, :2 * SPAN]
        diagonal = jnp.sum(skewed, axis=0)
        return jnp.take(diagonal, shifts + SPAN) * factor

    correlation = lax.map(one_row, lax.iota(jnp.int32, ROWS))
    return sinograms, correlation
```

```python
import functools
import math

import jax
import jax.numpy as jnp
from jax import lax
from jax.experimental import pallas as pl
from jax.experimental.pallas import tpu as pltpu
from jax.sharding import PartitionSpec as P

SPAN = 256
HALO = 16
GROUP = 4
TILE = 256
CELL = 128
VMEM_BYTES = 48 * 1024 * 1024

F32 = jnp.float32
BF16 = jnp.bfloat16


def call_params():
    return pltpu.CompilerParams(vmem_limit_bytes=VMEM_BYTES)


def whole(count):
    return [pl.BlockSpec(memory_space=pltpu.VMEM)] * count


def split_hi_lo(values):
    high = values.astype(BF16)
    return high, (values - high.astype(F32)).astype(BF16)


def banded(index, taps_ref, tap_count):
    total = jnp.zeros(index.shape, F32)
    for tap in range(tap_count):
        total = jnp.where(index == tap, taps_ref[tap], total)
    return total


def band_kernel(tap_count, rows, row_count, upper, share, place_ref, taps_ref, rowband_ref, colband_ref):
    me = place_ref[0]
    odd = lax.rem(me, 2)
    margin = tap_count // 2
    ext = rows + 2 * HALO
    height, depth = GROUP * rows, GROUP * ext
    out_at = lax.broadcasted_iota(jnp.int32, (height, depth), 0)
    in_at = lax.broadcasted_iota(jnp.int32, (height, depth), 1)
    line = out_at % share
    plane = (out_at // share) % GROUP
    block = out_at // (share * GROUP)
    step, up = block // upper, block % upper
    row = (up * row_count + (step ^ me)) * share + line
    place = in_at % ext
    straight = place - HALO
    crossed = jnp.where(place < HALO, rows + place, jnp.where(place >= rows + HALO, place - rows - 2 * HALO, straight))
    source = jnp.where(odd == 1, straight, crossed)
    index = jnp.where(in_at // ext == plane, source - row + margin, -1)
    high, low = split_hi_lo(banded(index, taps_ref, tap_count))
    rowband_ref[:height] = high
    rowband_ref[height:] = low
    width = TILE + 2 * CELL
    from_at = lax.broadcasted_iota(jnp.int32, (width, TILE), 0)
    to_at = lax.broadcasted_iota(jnp.int32, (width, TILE), 1)
    high, low = split_hi_lo(banded(from_at - CELL - to_at + margin, taps_ref, tap_count))
    colband_ref[0] = high
    colband_ref[1] = low


def lowpass_kernel(
    planes, rows, row_count, upper, share,
    place_ref, raw_ref, near_ref, far_ref, dark_ref, flat_ref, rowband_ref, colband_ref, *rest
):
    out_refs, (level_ref, dark_all_ref, absorbed_ref, high_ref, low_ref, smooth_ref) = rest[:row_count], rest[row_count:]
    cols = raw_ref.shape[-1]
    ext = rows + 2 * HALO
    far_ok = place_ref[1] == 1
    at = lax.broadcasted_iota(jnp.int32, (HALO, cols), 0)
    far_mask = (at * 0 + place_ref[1]) == 1
    spans = ((0, HALO), (HALO, rows), (HALO + rows, HALO))
    for (start, size), darkness, brightness in zip(
        spans,
        (near_ref[planes], dark_ref[...], far_ref[planes]),
        (near_ref[planes + 1], flat_ref[...], far_ref[planes + 1]),
    ):
        darkness = darkness.astype(F32)
        dark_all_ref[start : start + size] = darkness
        level_ref[start : start + size] = jnp.log(brightness.astype(F32) - darkness)
    for pad_ref in (high_ref, low_ref):
        pad_ref[:, :CELL] = jnp.zeros((pad_ref.shape[0], CELL), BF16)
        pad_ref[:, CELL + cols :] = jnp.zeros((pad_ref.shape[0], CELL), BF16)
    height = GROUP * rows
    for group in range(planes // GROUP):
        for inner in range(GROUP):
            plane = group * GROUP + inner
            for (start, size), counts_ref in zip(spans, (near_ref, raw_ref, far_ref)):
                counts = counts_ref[plane].astype(F32)
                absorbed = level_ref[start : start + size] - jnp.log(counts - dark_all_ref[start : start + size])
                if start > HALO:
                    absorbed = jnp.where(far_mask, absorbed, 0.0)
                absorbed_ref[inner * ext + start : inner * ext + start + size] = absorbed.astype(BF16)
        for at_col in range(0, cols, TILE):
            both = jnp.dot(rowband_ref[...], absorbed_ref[:, at_col : at_col + TILE], preferred_element_type=F32)
            high, low = split_hi_lo(both[:height] + both[height:])
            high_ref[:, CELL + at_col : CELL + at_col + TILE] = high
            low_ref[:, CELL + at_col : CELL + at_col + TILE] = low
        total = jnp.zeros((height, 1), F32)
        for at_col in range(0, cols, TILE):
            window = slice(at_col, at_col + TILE + 2 * CELL)
            piece = (
                jnp.dot(high_ref[:, window], colband_ref[0], preferred_element_type=F32)
                + jnp.dot(low_ref[:, window], colband_ref[0], preferred_element_type=F32)
                + jnp.dot(high_ref[:, window], colband_ref[1], preferred_element_type=F32)
            )
            smooth_ref[:, at_col : at_col + TILE] = piece
            total = total + jnp.sum(piece, axis=1, keepdims=True)
        mean = total / cols
        per_block = GROUP * share
        for step in range(row_count):
            for up in range(upper):
                start = (step * upper + up) * per_block
                centered = smooth_ref[start : start + per_block] - mean[start : start + per_block]
                out_refs[step][group, up] = centered.astype(BF16)


def lowpass(place, raw, near, far, dark, flat, rowband, colband, row_count, upper, share):
    planes, rows, cols = raw.shape
    ext = rows + 2 * HALO
    shape = jax.ShapeDtypeStruct((planes // GROUP, upper, GROUP * share, cols), BF16)
    height = GROUP * rows
    return pl.pallas_call(
        functools.partial(lowpass_kernel, planes, rows, row_count, upper, share),
        out_shape=[shape] * row_count,
        in_specs=[pl.BlockSpec(memory_space=pltpu.SMEM)] + whole(7),
        out_specs=whole(row_count),
        scratch_shapes=[
            pltpu.VMEM((ext, cols), F32),
            pltpu.VMEM((ext, cols), F32),
            pltpu.VMEM((GROUP * ext, cols), BF16),
            pltpu.VMEM((height, cols + 2 * CELL), BF16),
            pltpu.VMEM((height, cols + 2 * CELL), BF16),
            pltpu.VMEM((height, cols), F32),
        ],
        compiler_params=call_params(),
        cost_estimate=pl.CostEstimate(
            flops=2 * planes * rows * cols * 1500, bytes_accessed=planes * rows * cols * 6, transcendentals=planes * ext * cols
        ),
    )(place, raw, near, far, dark, flat, rowband, colband)


def ramp_kernel(cols, out_ref):
    steps = cols // TILE
    for block in range(2 * steps - 1):
        source = lax.broadcasted_iota(jnp.int32, (TILE, TILE), 0) + (block - (steps - 1)) * TILE
        distance = source - lax.broadcasted_iota(jnp.int32, (TILE, TILE), 1)
        spacing = distance.astype(F32)
        falloff = -4.0 / (math.pi * math.pi * jnp.maximum(spacing * spacing, 1.0))
        odd = (distance & 1) != 0
        values = jnp.where(distance == 0, 1.0, jnp.where(odd, falloff, 0.0))
        out_ref[block * TILE : (block + 1) * TILE] = values.astype(BF16)


def finish_kernel(half, share, pad_half, lines_ref, ramp_ref, partner_ref, shifts_ref, out_ref, corr_ref, lead_ref, mate_ref, ls_ref, ms_ref, prof_ref):
    count, cols = lines_ref.shape
    steps = cols // TILE
    for block in range(steps):
        start = (steps - 1 - block) * TILE
        panel = ramp_ref[start : start + cols]
        out_ref[:, block * TILE : (block + 1) * TILE] = jnp.dot(
            lines_ref[...], panel, preferred_element_type=F32
        ).astype(BF16)
    picks = share * pad_half
    pick_at = lax.broadcasted_iota(jnp.int32, (picks, count), 0)
    line_at = lax.broadcasted_iota(jnp.int32, (picks, count), 1)
    row, first = pick_at // pad_half, pick_at % pad_half
    wanted = jnp.where(first < half, first * share + row, -1)
    lead_pick = (line_at == wanted).astype(F32).astype(BF16)
    other = jnp.broadcast_to(partner_ref[...], (picks, count))
    wanted = jnp.where(other >= 0, other * share + row, -1)
    mate_pick = (line_at == wanted).astype(F32).astype(BF16)
    mate_ref[:, :SPAN] = jnp.zeros((picks, SPAN), BF16)
    mate_ref[:, SPAN + cols :] = jnp.zeros((picks, SPAN), BF16)
    for at_col in range(0, cols, TILE):
        piece = lines_ref[:, at_col : at_col + TILE]
        lead_ref[:, at_col : at_col + TILE] = jnp.dot(lead_pick, piece, preferred_element_type=F32).astype(BF16)
        mate_ref[:, SPAN + at_col : SPAN + at_col + TILE] = jnp.dot(
            mate_pick, piece, preferred_element_type=F32
        ).astype(BF16)
    cells = cols // CELL
    width = CELL + 2 * SPAN
    for row in range(share):
        lines = slice(row * pad_half, (row + 1) * pad_half)
        for cell in range(cells):
            ls_ref[cell * pad_half : (cell + 1) * pad_half] = lead_ref[lines, cell * CELL : (cell + 1) * CELL]
            back = (cells - 1 - cell) * CELL
            ms_ref[cell * pad_half : (cell + 1) * pad_half] = mate_ref[lines, back : back + width]
        products = lax.dot_general(
            ls_ref[...], ms_ref[...], (((0,), (0,)), ((), ())), preferred_element_type=F32
        )
        skewed = pltpu.roll(products, 0, 1, stride=1, stride_axis=0)
        prof_ref[row : row + 1] = jnp.sum(skewed[:, CELL:], axis=0, keepdims=True)
    number = shifts_ref.shape[1]
    at = lax.broadcasted_iota(jnp.int32, (2 * SPAN, number), 0)
    selector = (at == SPAN - 1 - shifts_ref[...]).astype(F32)
    picked = jnp.dot(prof_ref[...], selector, precision=lax.Precision.HIGHEST, preferred_element_type=F32)
    corr_ref[...] = picked * (half * cols) ** (-0.5)


def finish(lines, ramp, partner, shifts, share):
    count, cols = lines.shape
    half = partner.shape[0]
    pad_half = -(-half // 16) * 16
    padded = jnp.pad(partner, (0, pad_half - half), constant_values=-1)
    partner_column = jnp.tile(padded, share)[:, None]
    cells = cols // CELL
    return pl.pallas_call(
        functools.partial(finish_kernel, half, share, pad_half),
        out_shape=[
            jax.ShapeDtypeStruct((count, cols), BF16),
            jax.ShapeDtypeStruct((share, shifts.shape[0]), F32),
        ],
        in_specs=whole(4),
        out_specs=whole(2),
        scratch_shapes=[
            pltpu.VMEM((share * pad_half, cols), BF16),
            pltpu.VMEM((share * pad_half, cols + 2 * SPAN), BF16),
            pltpu.VMEM((cells * pad_half, CELL), BF16),
            pltpu.VMEM((cells * pad_half, CELL + 2 * SPAN), BF16),
            pltpu.VMEM((share, 2 * SPAN), F32),
        ],
        compiler_params=call_params(),
    )(lines, ramp, partner_column, shifts[None, :])


def shards(raw_frames, dark_field, flat_field, kernel_taps, partner, shifts):
    planes, rows, cols = raw_frames.shape
    tap_count = kernel_taps.shape[0]
    row_count, ang_count = lax.axis_size("row"), lax.axis_size("ang")
    upper, share = ang_count // row_count, rows // ang_count
    me, turn = lax.axis_index("row"), lax.axis_index("ang")
    odd = me % 2
    inner = jnp.logical_and(me > 0, me < row_count - 1)
    place = jnp.stack([me, inner.astype(jnp.int32)]).astype(jnp.int32)

    def edge(start):
        parts = [raw_frames, dark_field[None], flat_field[None]]
        return jnp.concatenate([lax.dynamic_slice_in_dim(part, start, HALO, 1) for part in parts])

    near = lax.ppermute(edge(jnp.where(odd == 1, 0, rows - HALO)), "row", [(i, i ^ 1) for i in range(row_count)])
    cross = [(i, i + 1) for i in range(1, row_count - 1, 2)]
    far = lax.ppermute(
        edge(jnp.where(odd == 1, rows - HALO, 0)), "row", cross + [(j, i) for i, j in cross]
    )
    ext = rows + 2 * HALO
    rowband, colband = pl.pallas_call(
        functools.partial(band_kernel, tap_count, rows, row_count, upper, share),
        out_shape=[
            jax.ShapeDtypeStruct((2 * GROUP * rows, GROUP * ext), BF16),
            jax.ShapeDtypeStruct((2, TILE + 2 * CELL, TILE), BF16),
        ],
        in_specs=[pl.BlockSpec(memory_space=pltpu.SMEM)] * 2,
        out_specs=whole(2),
        compiler_params=call_params(),
    )(place, kernel_taps)
    ramp = pl.pallas_call(
        functools.partial(ramp_kernel, cols),
        out_shape=jax.ShapeDtypeStruct(((2 * (cols // TILE) - 1) * TILE, TILE), BF16),
        out_specs=whole(1)[0],
        compiler_params=call_params(),
    )()
    sent = lowpass(place, raw_frames, near, far, dark_field, flat_field, rowband, colband, row_count, upper, share)
    held = [sent[0]]
    for step in range(1, row_count):
        held.append(lax.ppermute(sent[step], "row", [(i, i ^ step) for i in range(row_count)]))
    held = jnp.stack(held)
    lines = jnp.zeros((ang_count,) + held.shape[1:2] + held.shape[3:], BF16)
    for step in range(ang_count):
        target = turn ^ step
        piece = lax.dynamic_slice(
            held,
            (me ^ (target // upper), 0, target % upper, 0, 0),
            (1, held.shape[1], 1, held.shape[3], cols),
        ).reshape(lines.shape[1:])
        if step:
            piece = lax.ppermute(piece, "ang", [(i, i ^ step) for i in range(ang_count)])
        lines = lax.dynamic_update_slice_in_dim(lines, piece[None], turn ^ step, 0)
    filtered, correlation = finish(lines.reshape(-1, cols), ramp, partner, shifts, share)
    return filtered.reshape(-1, share, cols), correlation


def solution(mesh):
    in_specs = (
        P(("scan", "ang"), "row", None),
        P("row", None),
        P("row", None),
        P(),
        P("scan"),
        P(),
    )
    out_specs = (P("scan", ("ang", "row"), None), P(("scan", "ang", "row"), None))
    return jax.shard_map(shards, mesh=mesh, in_specs=in_specs, out_specs=out_specs, check_vma=False)
```

```python
import functools
import math

import jax
import jax.numpy as jnp
from jax import lax
from jax.experimental import pallas as pl
from jax.experimental.pallas import tpu as pltpu
from jax.sharding import PartitionSpec as P

SPAN = 256
HALO = 16
GROUP = 4
TILE = 256
CELL = 128
VMEM_BYTES = 24 * 1024 * 1024

F32 = jnp.float32
BF16 = jnp.bfloat16


def call_params():
    return pltpu.CompilerParams(vmem_limit_bytes=VMEM_BYTES)


def whole(count):
    return [pl.BlockSpec(memory_space=pltpu.VMEM)] * count


def anywhere(count):
    return [pl.BlockSpec(memory_space=pl.ANY)] * count


def cost(micros):
    return pl.CostEstimate(flops=int(micros * 1.15e9), bytes_accessed=1 << 16, transcendentals=0)


def skipping(kernel, at, count=1):
    return lambda *refs: kernel(*refs[:at], *refs[at + count :])


def split_hi_lo(values):
    high = values.astype(BF16)
    return high, (values - high.astype(F32)).astype(BF16)


def banded(index, taps_ref, tap_count):
    total = jnp.zeros(index.shape, F32)
    for tap in range(tap_count):
        total = jnp.where(index == tap, taps_ref[tap], total)
    return total


def pick_kernel(planes, half, pad_half, share, place_ref, partner_ref, pick_ref):
    turn = place_ref[2]
    picks, count = pick_ref.shape[0] // 2, pick_ref.shape[1]
    pick_at = lax.broadcasted_iota(jnp.int32, (picks, 1), 0)
    row, first = pick_at // pad_half, pick_at % pad_half
    lead_at = jnp.full((picks, 1), -1, jnp.int32)
    mate_at = lead_at

    def stands(plane):
        step = turn ^ (plane // planes)
        return (step * planes + plane % planes) * share

    for plane in range(half):
        here = first == plane
        lead_at = jnp.where(here, stands(plane) + row, lead_at)
        mate_at = jnp.where(here, stands(partner_ref[plane]) + row, mate_at)
    line_at = lax.broadcasted_iota(jnp.int32, (picks, count), 1)
    pick_ref[:picks] = (line_at == lead_at).astype(F32).astype(BF16)
    pick_ref[picks:] = (line_at == mate_at).astype(F32).astype(BF16)


def band_kernel(tap_count, rows, row_count, upper, share, place_ref, taps_ref, rowband_ref, colband_ref):
    me = place_ref[0]
    odd = lax.rem(me, 2)
    margin = tap_count // 2
    ext = rows + 2 * HALO
    height, depth = GROUP * rows, GROUP * ext
    out_at = lax.broadcasted_iota(jnp.int32, (height, depth), 0)
    in_at = lax.broadcasted_iota(jnp.int32, (height, depth), 1)
    line = out_at % share
    plane = (out_at // share) % GROUP
    block = out_at // (share * GROUP)
    step, up = block // upper, block % upper
    row = (up * row_count + (step ^ me)) * share + line
    place = in_at % ext
    straight = place - HALO
    crossed = jnp.where(place < HALO, rows + place, jnp.where(place >= rows + HALO, place - rows - 2 * HALO, straight))
    source = jnp.where(odd == 1, straight, crossed)
    index = jnp.where(in_at // ext == plane, source - row + margin, -1)
    high, low = split_hi_lo(banded(index, taps_ref, tap_count))
    rowband_ref[:height] = high
    rowband_ref[height:] = low
    width = TILE + 2 * CELL
    from_at = lax.broadcasted_iota(jnp.int32, (width, TILE), 0)
    lane = lax.broadcasted_iota(jnp.int32, (width, TILE), 1)
    to_at = jnp.where(lane < CELL, 2 * lane, 2 * (lane - CELL) + 1)
    high, low = split_hi_lo(banded(from_at - CELL - to_at + margin, taps_ref, tap_count))
    colband_ref[0] = high
    colband_ref[1] = low


def edge_kernel(planes, rows, crossing, place_ref, raw_ref, dark_ref, flat_ref, out_ref, sems):
    odd = lax.rem(place_ref[0], 2)
    span = pl.ds(pl.multiple_of((odd if crossing else 1 - odd) * (rows - HALO), HALO), HALO)
    copies = [
        pltpu.make_async_copy(raw_ref.at[:, span], out_ref.at[:planes], sems.at[0]),
        pltpu.make_async_copy(dark_ref.at[span], out_ref.at[planes], sems.at[1]),
        pltpu.make_async_copy(flat_ref.at[span], out_ref.at[planes + 1], sems.at[2]),
    ]
    for copy in copies:
        copy.start()
    for copy in copies:
        copy.wait()


def edge(place, raw, dark, flat, crossing, after):
    planes, rows, cols = raw.shape
    return pl.pallas_call(
        skipping(functools.partial(edge_kernel, planes, rows, crossing), 4, len(after)),
        out_shape=jax.ShapeDtypeStruct((planes + 2, HALO, cols), BF16),
        in_specs=[pl.BlockSpec(memory_space=pltpu.SMEM)] + anywhere(3 + len(after)),
        out_specs=whole(1)[0],
        scratch_shapes=[pltpu.SemaphoreType.DMA((3,))],
        cost_estimate=cost(2.0),
    )(place, raw, dark, flat, *after)


def lowpass_kernel(
    rows, row_count, upper, share, wants_inner,
    place_ref, raw_ref, near_ref, far_ref, near_field_ref, far_field_ref, dark_ref, flat_ref, rowband_ref, colband_ref, *rest
):
    out_refs, (level_ref, dark_all_ref, absorbed_ref, high_ref, low_ref, smooth_ref) = rest[:row_count], rest[row_count:]
    cols = raw_ref.shape[-1]
    ext = rows + 2 * HALO
    height = GROUP * rows
    active = place_ref[1] == wants_inner
    spans = ((0, HALO), (HALO, rows), (HALO + rows, HALO))

    @pl.when(jnp.logical_and(active, pl.program_id(0) == 0))
    def _():
        for (start, size), darkness, brightness in zip(
            spans,
            (near_field_ref[0], dark_ref[...], far_field_ref[0]),
            (near_field_ref[1], flat_ref[...], far_field_ref[1]),
        ):
            darkness = darkness.astype(F32)
            dark_all_ref[start : start + size] = darkness
            level_ref[start : start + size] = jnp.log(brightness.astype(F32) - darkness)
        for pad_ref in (high_ref, low_ref):
            pad_ref[:, :CELL] = jnp.zeros((height, CELL), BF16)
            pad_ref[:, CELL + cols :] = jnp.zeros((height, CELL), BF16)

    @pl.when(active)
    def _():
        for plane in range(GROUP):
            for (start, size), counts_ref in zip(spans, (near_ref, raw_ref, far_ref)):
                place = plane * ext + start
                if start > HALO and not wants_inner:
                    absorbed_ref[place : place + size] = jnp.zeros((size, cols), BF16)
                    continue
                counts = counts_ref[plane].astype(F32)
                absorbed = level_ref[start : start + size] - jnp.log(counts - dark_all_ref[start : start + size])
                absorbed_ref[place : place + size] = absorbed.astype(BF16)
        for at_col in range(0, cols, TILE):
            both = jnp.dot(rowband_ref[...], absorbed_ref[:, at_col : at_col + TILE], preferred_element_type=F32)
            high, low = split_hi_lo(both[:height] + both[height:])
            high_ref[:, CELL + at_col : CELL + at_col + TILE] = high
            low_ref[:, CELL + at_col : CELL + at_col + TILE] = low
        total = jnp.zeros((height, 1), F32)
        for at_col in range(0, cols, TILE):
            window = slice(at_col, at_col + TILE + 2 * CELL)
            piece = (
                jnp.dot(high_ref[:, window], colband_ref[0], preferred_element_type=F32)
                + jnp.dot(low_ref[:, window], colband_ref[0], preferred_element_type=F32)
                + jnp.dot(high_ref[:, window], colband_ref[1], preferred_element_type=F32)
            )
            at_half = at_col // 2
            smooth_ref[:, at_half : at_half + CELL] = piece[:, :CELL]
            smooth_ref[:, cols // 2 + at_half : cols // 2 + at_half + CELL] = piece[:, CELL:]
            total = total + jnp.sum(piece, axis=1, keepdims=True)
        mean = total / cols
        per_block = GROUP * share
        for step in range(row_count):
            for up in range(upper):
                start = (step * upper + up) * per_block
                centered = smooth_ref[start : start + per_block] - mean[start : start + per_block]
                out_refs[step][0, up] = centered.astype(BF16)


def lowpass(place, raw, near, far, dark, flat, rowband, colband, row_count, upper, share, wants_inner, first, groups, after):
    planes, rows, cols = raw.shape
    ext = rows + 2 * HALO
    shape = jax.ShapeDtypeStruct((groups, upper, GROUP * share, cols), BF16)
    height = GROUP * rows
    taken = lambda size: pl.BlockSpec((GROUP, size, cols), lambda group: (group + first, 0, 0))
    fields = pl.BlockSpec((2, HALO, cols), lambda group: (planes // 2, 0, 0))
    return pl.pallas_call(
        skipping(functools.partial(lowpass_kernel, rows, row_count, upper, share, wants_inner), 10, len(after)),
        grid=(groups,),
        out_shape=[shape] * row_count,
        in_specs=[pl.BlockSpec(memory_space=pltpu.SMEM), taken(rows), taken(HALO), taken(HALO), fields, fields] + whole(4) + anywhere(len(after)),
        out_specs=[pl.BlockSpec((1, upper, GROUP * share, cols), lambda group: (group, 0, 0, 0))] * row_count,
        scratch_shapes=[
            pltpu.VMEM((ext, cols), F32),
            pltpu.VMEM((ext, cols), F32),
            pltpu.VMEM((GROUP * ext, cols), BF16),
            pltpu.VMEM((height, cols + 2 * CELL), BF16),
            pltpu.VMEM((height, cols + 2 * CELL), BF16),
            pltpu.VMEM((height, cols), F32),
        ],
        compiler_params=call_params(),
        cost_estimate=cost(2.7 * groups),
    )(place, raw, near, far, near, far, dark, flat, rowband, colband, *after)


def route_kernel(row_count, ang_count, upper, place_ref, *rest):
    slots, targets, sems = rest[:row_count], rest[row_count:-1], rest[-1]
    me, turn = place_ref[0], place_ref[2]
    for step in range(1, ang_count):
        target = turn ^ step
        slot = me ^ (target // upper)
        for number in range(row_count):

            @pl.when(slot == number)
            def _():
                pltpu.make_async_copy(slots[number].at[:, target % upper], targets[step - 1], sems.at[step]).start()

    for step in range(1, ang_count):
        pltpu.make_async_copy(slots[0].at[:, 0], targets[step - 1], sems.at[step]).wait()


def route(place, slots, ang_count, after):
    groups, upper, lines, cols = slots[0].shape
    return pl.pallas_call(
        skipping(functools.partial(route_kernel, len(slots), ang_count, upper), 1 + len(slots)),
        out_shape=[jax.ShapeDtypeStruct((groups, lines, cols), BF16)] * (ang_count - 1),
        in_specs=[pl.BlockSpec(memory_space=pltpu.SMEM)] + anywhere(len(slots) + 1),
        out_specs=whole(ang_count - 1),
        scratch_shapes=[pltpu.SemaphoreType.DMA((ang_count,))],
        cost_estimate=cost(2.0),
    )(place, *slots, after)


def ramp_kernel(cols, to_even_ref, to_odd_ref, weave_ref):
    steps = cols // (2 * TILE)
    for out_ref, parity in ((to_even_ref, 1), (to_odd_ref, -1)):
        for block in range(2 * steps - 1):
            source = lax.broadcasted_iota(jnp.int32, (TILE, TILE), 0) + (block - (steps - 1)) * TILE
            distance = 2 * (source - lax.broadcasted_iota(jnp.int32, (TILE, TILE), 1)) + parity
            spacing = distance.astype(F32)
            falloff = -4.0 / (math.pi * math.pi * (spacing * spacing))
            out_ref[block * TILE : (block + 1) * TILE] = falloff.astype(BF16)
    source = lax.broadcasted_iota(jnp.int32, (TILE, TILE), 0)
    target = lax.broadcasted_iota(jnp.int32, (TILE, TILE), 1)
    place = jnp.where(source < CELL, 2 * source, 2 * (source - CELL) + 1)
    weave_ref[...] = (place == target).astype(F32).astype(BF16)


def ramp_lines(lines, to_even_ref, to_odd_ref, weave_ref, store):
    half = lines.shape[1] // 2
    steps = half // TILE
    for block in range(steps):
        rows = slice((steps - 1 - block) * TILE, (steps - 1 - block) * TILE + half)
        here = slice(block * TILE, (block + 1) * TILE)
        even = lines[:, here].astype(F32) + jnp.dot(
            lines[:, half:], to_even_ref[rows], preferred_element_type=F32
        )
        odd = lines[:, half + block * TILE : half + (block + 1) * TILE].astype(F32) + jnp.dot(
            lines[:, :half], to_odd_ref[rows], preferred_element_type=F32
        )
        even, odd = even.astype(BF16), odd.astype(BF16)
        for part in range(TILE // CELL):
            span = slice(part * CELL, (part + 1) * CELL)
            both = jnp.concatenate([even[:, span], odd[:, span]], axis=1)
            store(
                (TILE // CELL) * block + part, jnp.dot(both, weave_ref[...], preferred_element_type=F32).astype(BF16)
            )


def correlate(share, pad_half, scale, lines, pick_ref, shifts_ref, corr_ref, lead_ref, mate_ref, ls_ref, ms_ref, prof_ref):
    count, cols = lines.shape
    half, reach = cols // 2, SPAN // 2
    padded, width = half + 2 * reach, CELL + 2 * reach
    picks = share * pad_half
    for parity in range(2):
        start = parity * padded
        mate_ref[:, start : start + reach] = jnp.zeros((picks, reach), BF16)
        mate_ref[:, start + reach + half : start + padded] = jnp.zeros((picks, reach), BF16)
        for at_col in range(0, half, TILE):
            here = parity * half + at_col
            picked = jnp.dot(pick_ref[...], lines[:, here : here + TILE], preferred_element_type=F32).astype(BF16)
            lead_ref[:, here : here + TILE] = picked[:picks]
            place = start + reach + at_col
            mate_ref[:, place : place + TILE] = picked[picks:]
    cells = half // CELL
    for row in range(share):
        span = slice(row * pad_half, (row + 1) * pad_half)
        for cell in range(cells):
            stack = slice(cell * pad_half, (cell + 1) * pad_half)
            back = (cells - 1 - cell) * CELL
            for parity in range(2):
                at = parity * half + cell * CELL
                ls_ref[stack, parity * CELL : (parity + 1) * CELL] = lead_ref[span, at : at + CELL]
                at = parity * padded + back
                ms_ref[stack, parity * width : (parity + 1) * width] = mate_ref[span, at : at + width]
        products = lax.dot_general(ls_ref[...], ms_ref[...], (((0,), (0,)), ((), ())), preferred_element_type=F32)
        tables = (
            products[:CELL, :width],
            products[CELL:, width:],
            products[:CELL, width:] + products[CELL:, :width],
        )
        for number, table in enumerate(tables):
            skewed = pltpu.roll(table, 0, 1, stride=1, stride_axis=0)
            prof_ref[row : row + 1, number * width : (number + 1) * width] = jnp.sum(skewed, axis=0, keepdims=True)
    shifts = shifts_ref[...]
    middle = CELL + reach - 1 - lax.shift_right_arithmetic(shifts, 1)
    odd = (shifts & 1) == 1
    wanted = (jnp.where(odd, middle, -1), jnp.where(odd, middle - 1, -1), jnp.where(odd, -1, middle))
    at = lax.broadcasted_iota(jnp.int32, (width, shifts.shape[1]), 0)
    total = jnp.zeros(corr_ref.shape, F32)
    for number, place in enumerate(wanted):
        selector = (at == place).astype(F32).astype(BF16)
        rest = prof_ref[:, number * width : (number + 1) * width]
        for _ in range(3):
            high = rest.astype(BF16)
            total = total + jnp.dot(high, selector, preferred_element_type=F32)
            rest = rest - high.astype(F32)
    corr_ref[...] = total * scale


def finish_kernel(upper, slot_count, ang_count, wants_inner, has_out, has_corr, share, pad_half, scale, *refs):
    refs = list(refs)
    take = lambda count: [refs.pop(0) for _ in range(count)]
    place_ref, *ramp_refs = take(4)
    slots, pieces, (pick_ref, shifts_ref) = take(slot_count), take(ang_count - 1), take(2)
    take(1 if has_out else 0)
    (old_corr_ref,) = take(1) if has_corr else (None,)
    out_ref, corr_ref, x_ref, y_ref, in_sems, out_sems = take(6)
    me, turn = place_ref[0], place_ref[2]
    active = place_ref[3] == wants_inner
    groups = x_ref.shape[0] // ang_count

    @pl.when(active)
    def _():
        for number, slot in enumerate(slots):

            @pl.when(me ^ (turn // upper) == number)
            def _():
                pltpu.make_async_copy(slot.at[:, turn % upper], x_ref.at[:groups], in_sems.at[0]).start()

        copies = [pltpu.make_async_copy(slots[0].at[:, 0], x_ref.at[:groups], in_sems.at[0])]
        for step in range(1, ang_count):
            target = x_ref.at[step * groups : (step + 1) * groups]
            copies.append(pltpu.make_async_copy(pieces[step - 1], target, in_sems.at[step]))
            copies[-1].start()
        for copy in copies:
            copy.wait()
        stands, lines_each, cols = x_ref.shape
        lines = x_ref[...].reshape(stands * lines_each, cols)

        def store(block, values):
            y_ref[:, :, block * TILE : (block + 1) * TILE] = values.reshape(stands, lines_each, TILE)

        ramp_lines(lines, *ramp_refs, store)
        outs = []
        for step in range(ang_count):
            target = out_ref.at[pl.ds((turn ^ step) * groups, groups)]
            outs.append(
                pltpu.make_async_copy(y_ref.at[step * groups : (step + 1) * groups], target, out_sems.at[step])
            )
            outs[-1].start()
        correlate(share, pad_half, scale, lines, pick_ref, shifts_ref, corr_ref, *refs)
        for copy in outs:
            copy.wait()

    @pl.when(jnp.logical_not(active))
    def _():
        corr_ref[...] = old_corr_ref[...] if has_corr else jnp.zeros(corr_ref.shape, F32)


def finish(place, ramp, slots, pieces, picks, out, corr, wants_inner, upper, share, half, after):
    ang_count = len(pieces) + 1
    groups, lines_each, cols = pieces[0].shape
    pad_half = padded_half(half)
    args = [place, *ramp, *slots, *pieces, *picks]
    specs = [pl.BlockSpec(memory_space=pltpu.SMEM)] + whole(3) + anywhere(len(slots) + len(pieces)) + whole(2)
    cells, width = cols // (2 * CELL), CELL + SPAN
    aliases = {}
    if out is not None:
        aliases[len(args)] = 0
        args, specs = args + [out], specs + anywhere(1)
    if corr is not None:
        args, specs = args + [corr], specs + whole(1)
    args, specs = args + [after], specs + anywhere(1)
    kernel = functools.partial(
        finish_kernel, upper, len(slots), ang_count, wants_inner, out is not None, corr is not None, share, pad_half,
        (half * cols) ** (-0.5),
    )
    return pl.pallas_call(
        skipping(kernel, len(args) - 1),
        out_shape=[
            jax.ShapeDtypeStruct((ang_count * groups, lines_each, cols), BF16),
            jax.ShapeDtypeStruct((share, picks[1].shape[1]), F32),
        ],
        in_specs=specs,
        out_specs=anywhere(1) + whole(1),
        scratch_shapes=[
            pltpu.VMEM((groups * ang_count, lines_each, cols), BF16),
            pltpu.VMEM((groups * ang_count, lines_each, cols), BF16),
            pltpu.SemaphoreType.DMA((ang_count,)),
            pltpu.SemaphoreType.DMA((ang_count,)),
            pltpu.VMEM((share * pad_half, cols), BF16),
            pltpu.VMEM((share * pad_half, cols + 2 * SPAN), BF16),
            pltpu.VMEM((cells * pad_half, 2 * CELL), BF16),
            pltpu.VMEM((cells * pad_half, 2 * width), BF16),
            pltpu.VMEM((share, 3 * width), F32),
        ],
        input_output_aliases=aliases,
        compiler_params=call_params(),
        cost_estimate=cost(8.0),
    )(*args)


def padded_half(half):
    return -(-half // 16) * 16


def shards(raw_frames, dark_field, flat_field, kernel_taps, partner, shifts):
    planes, rows, cols = raw_frames.shape
    tap_count = kernel_taps.shape[0]
    half = partner.shape[0]
    row_count, ang_count = lax.axis_size("row"), lax.axis_size("ang")
    upper, share = ang_count // row_count, rows // ang_count
    me, turn = lax.axis_index("row"), lax.axis_index("ang")
    is_inner = lambda at: jnp.logical_and(at > 0, at < row_count - 1).astype(jnp.int32)
    place = jnp.stack([me, is_inner(me), turn, is_inner(turn // upper)]).astype(jnp.int32)

    cross = [(i, i + 1) for i in range(1, row_count - 1, 2)]
    far = edge(place, raw_frames, dark_field, flat_field, True, [])
    near = edge(place, raw_frames, dark_field, flat_field, False, [far])
    far = lax.ppermute(far, "row", cross + [(j, i) for i, j in cross])
    near = lax.ppermute(near, "row", [(i, i ^ 1) for i in range(row_count)])
    ext = rows + 2 * HALO
    rowband, colband = pl.pallas_call(
        functools.partial(band_kernel, tap_count, rows, row_count, upper, share),
        out_shape=[
            jax.ShapeDtypeStruct((2 * GROUP * rows, GROUP * ext), BF16),
            jax.ShapeDtypeStruct((2, TILE + 2 * CELL, TILE), BF16),
        ],
        in_specs=[pl.BlockSpec(memory_space=pltpu.SMEM)] * 2,
        out_specs=whole(2),
        compiler_params=call_params(),
        cost_estimate=cost(2.0),
    )(place, kernel_taps)
    ramp = pl.pallas_call(
        functools.partial(ramp_kernel, cols),
        out_shape=[jax.ShapeDtypeStruct((cols - TILE, TILE), BF16)] * 2 + [jax.ShapeDtypeStruct((TILE, TILE), BF16)],
        out_specs=whole(3),
        compiler_params=call_params(),
        cost_estimate=cost(1.8),
    )()

    total = planes // GROUP
    pad_half = padded_half(half)

    pick = pl.pallas_call(
        functools.partial(pick_kernel, planes, half, pad_half, share),
        out_shape=jax.ShapeDtypeStruct((2 * share * pad_half, ang_count * planes * share), BF16),
        in_specs=[pl.BlockSpec(memory_space=pltpu.SMEM)] * 2,
        out_specs=whole(1)[0],
        compiler_params=call_params(),
        cost_estimate=cost(1.5),
    )(place, partner)
    picks = (pick, shifts[None, :])

    ends = (0, row_count - 1)
    mine = lambda inner, source: (source in ends) != bool(inner)

    def filter_rows(inner, after):
        sent = lowpass(
            place, raw_frames, near, far if inner else near, dark_field, flat_field, rowband, colband,
            row_count, upper, share, inner, 0, total, after,
        )
        slots = [sent[0]]
        for step in range(1, row_count):
            pairs = [(i, i ^ step) for i in range(row_count) if mine(inner, i)]
            slots.append(lax.ppermute(sent[step], "row", pairs))
        return slots

    def regroup(inner, slots, after):
        pieces = list(route(place, slots, ang_count, after))
        for step in range(1, ang_count):
            pairs = [(i, i ^ step) for i in range(ang_count) if mine(inner, (i ^ step) // upper)]
            pieces[step - 1] = lax.ppermute(pieces[step - 1], "ang", pairs)
        return pieces

    outer = filter_rows(0, [])
    inner = filter_rows(1, [outer[0], ramp[0], pick])
    outer_lines = regroup(0, outer, inner[0])
    inner_lines = regroup(1, inner, inner[0])
    out, corr = finish(place, ramp, outer, outer_lines, picks, None, None, 0, upper, share, half, inner[0])
    filtered, correlation = finish(place, ramp, inner, inner_lines, picks, out, corr, 1, upper, share, half, corr)
    return filtered.reshape(-1, share, cols), correlation


def solution(mesh):
    in_specs = (
        P(("scan", "ang"), "row", None),
        P("row", None),
        P("row", None),
        P(),
        P("scan"),
        P(),
    )
    out_specs = (P("scan", ("ang", "row"), None), P(("scan", "ang", "row"), None))
    return jax.shard_map(shards, mesh=mesh, in_specs=in_specs, out_specs=out_specs, check_vma=False)
```

```python
import functools
import math

import jax
import jax.numpy as jnp
from jax import lax
from jax.experimental import pallas as pl
from jax.experimental.pallas import tpu as pltpu
from jax.sharding import PartitionSpec as P

SPAN = 256
HALO = 16
GROUP = 4
TILE = 256
CELL = 128
UNROLL = 2

F32 = jnp.float32
BF16 = jnp.bfloat16


def call_params(mebibytes=16):
    return pltpu.CompilerParams(vmem_limit_bytes=mebibytes << 20)


def whole(count):
    return [pl.BlockSpec(memory_space=pltpu.VMEM)] * count


def anywhere(count):
    return [pl.BlockSpec(memory_space=pl.ANY)] * count


def cost(micros):
    return pl.CostEstimate(flops=int(micros * 1.15e9), bytes_accessed=1 << 16, transcendentals=0)


def skipping(kernel, at, count=1):
    return lambda *refs: kernel(*refs[:at], *refs[at + count :])


def split_hi_lo(values):
    high = values.astype(BF16)
    return high, (values - high.astype(F32)).astype(BF16)


def banded(index, taps_ref, tap_count):
    total = jnp.zeros(index.shape, F32)
    for tap in range(tap_count):
        total = jnp.where(index == tap, taps_ref[tap], total)
    return total


def late_lanes(ang_count):
    return max(1, ang_count // 4)


def lane_width(lines):
    return -(-lines // CELL) * CELL


def pair_slots(half):
    return -(-(half // 2 + 1) // 16) * 16


def pick_kernel(planes, half, slots, share, place_ref, partner_ref, *pick_refs):
    turn = place_ref[2]
    picks = share * slots
    pick_at = lax.broadcasted_iota(jnp.int32, (picks, 1), 0)
    row, first = pick_at // slots, pick_at % slots
    lanes_early = pick_refs[0].shape[1]
    leads = [jnp.full((picks, 1), -1, jnp.int32) for _ in pick_refs]
    mates = list(leads)
    counts = [jnp.int32(0) for _ in pick_refs]

    def stands(plane):
        return (turn ^ (plane // planes)) * lane_width(planes * share) + plane % planes * share

    for plane in range(half):
        lead, mate = stands(plane), stands(partner_ref[plane])
        late = jnp.maximum(lead, mate) >= lanes_early
        for part, mine in enumerate((jnp.logical_not(late), late)):
            here = first == jnp.where(mine, counts[part], -1)
            leads[part] = jnp.where(here, lead + row, leads[part])
            mates[part] = jnp.where(here, mate + row, mates[part])
            counts[part] = counts[part] + jnp.where(mine, 1, 0)
    for part, pick_ref in enumerate(pick_refs):
        line_at = lax.broadcasted_iota(jnp.int32, (picks, pick_ref.shape[1]), 1)
        pick_ref[:picks] = (line_at == leads[part]).astype(F32).astype(BF16)
        pick_ref[picks:] = (line_at == mates[part]).astype(F32).astype(BF16)


def band_kernel(tap_count, rows, row_count, upper, share, place_ref, taps_ref, rowband_ref, colband_ref):
    me = place_ref[0]
    odd = lax.rem(me, 2)
    margin = tap_count // 2
    ext = rows + 2 * HALO
    height, depth = GROUP * rows, GROUP * ext
    out_at = lax.broadcasted_iota(jnp.int32, (height, depth), 0)
    in_at = lax.broadcasted_iota(jnp.int32, (height, depth), 1)
    line = out_at % share
    plane = (out_at // share) % GROUP
    block = out_at // (share * GROUP)
    step, up = block // upper, block % upper
    row = (up * row_count + (step ^ me)) * share + line
    place = in_at % ext
    straight = place - HALO
    crossed = jnp.where(place < HALO, rows + place, jnp.where(place >= rows + HALO, place - rows - 2 * HALO, straight))
    source = jnp.where(odd == 1, straight, crossed)
    index = jnp.where(in_at // ext == plane, source - row + margin, -1)
    high, low = split_hi_lo(banded(index, taps_ref, tap_count))
    rowband_ref[:height] = high
    rowband_ref[height:] = low
    width = TILE + 2 * CELL
    from_at = lax.broadcasted_iota(jnp.int32, (width, TILE), 0)
    lane = lax.broadcasted_iota(jnp.int32, (width, TILE), 1)
    to_at = jnp.where(lane < CELL, 2 * lane, 2 * (lane - CELL) + 1)
    high, low = split_hi_lo(banded(from_at - CELL - to_at + margin, taps_ref, tap_count))
    colband_ref[0] = high
    colband_ref[1] = low


def edge_kernel(planes, rows, place_ref, raw_ref, dark_ref, flat_ref, near_ref, far_ref, held_ref, in_sems, out_sems):
    odd = lax.rem(place_ref[0], 2)
    near_at = pl.multiple_of((1 - odd) * (rows - HALO), HALO)
    far_at = pl.multiple_of(odd * (rows - HALO), HALO)
    loads, stores = [], []
    for side, (out_ref, start) in enumerate(((far_ref, far_at), (near_ref, near_at))):
        span, held = pl.ds(start, HALO), held_ref.at[side]
        loads.append(
            [
                pltpu.make_async_copy(raw_ref.at[:, span], held.at[:planes], in_sems.at[side, 0]),
                pltpu.make_async_copy(dark_ref.at[span], held.at[planes], in_sems.at[side, 1]),
                pltpu.make_async_copy(flat_ref.at[span], held.at[planes + 1], in_sems.at[side, 2]),
            ]
        )
        stores.append(pltpu.make_async_copy(held, out_ref, out_sems.at[side]))
    for side in loads:
        for copy in side:
            copy.start()
    for side, store in zip(loads, stores):
        for copy in side:
            copy.wait()
        store.start()
    for store in stores:
        store.wait()


def edges(place, raw, dark, flat):
    planes, rows, cols = raw.shape
    return pl.pallas_call(
        functools.partial(edge_kernel, planes, rows),
        out_shape=[jax.ShapeDtypeStruct((planes + 2, HALO, cols), BF16)] * 2,
        in_specs=[pl.BlockSpec(memory_space=pltpu.SMEM)] + anywhere(3),
        out_specs=anywhere(2),
        scratch_shapes=[
            pltpu.VMEM((2, planes + 2, HALO, cols), BF16),
            pltpu.SemaphoreType.DMA((2, 3)),
            pltpu.SemaphoreType.DMA((2,)),
        ],
        compiler_params=call_params(60),
        cost_estimate=cost(2.0),
    )(place, raw, dark, flat)


def lowpass_kernel(
    groups, row_count, upper, share, wants_inner,
    place_ref, raw_ref, near_ref, far_ref, dark_ref, flat_ref, rowband_ref, colband_ref, *rest
):
    out_refs, (level_ref, dark_all_ref, absorbed_ref, held_ref, smooth_ref) = rest[:row_count], rest[row_count:]
    planes, rows, cols = raw_ref.shape
    ext = rows + 2 * HALO
    height = GROUP * rows
    per_block = GROUP * share
    spans = ((0, HALO), (HALO, rows), (HALO + rows, HALO))

    @pl.when(place_ref[1] == wants_inner)
    def _():
        fields = (
            (near_ref[planes], near_ref[planes + 1]),
            (dark_ref[...], flat_ref[...]),
            (far_ref[planes], far_ref[planes + 1]),
        )
        for (start, size), (darkness, brightness) in zip(spans, fields):
            darkness = darkness.astype(F32)
            dark_all_ref[start : start + size] = darkness
            level_ref[start : start + size] = jnp.log(brightness.astype(F32) - darkness)
        for group in range(groups):
            sums = []
            for inner in range(GROUP):
                for (start, size), counts_ref in zip(spans, (near_ref, raw_ref, far_ref)):
                    place = inner * ext + start
                    if start > HALO and not wants_inner:
                        absorbed_ref[place : place + size] = jnp.zeros((size, cols), BF16)
                        sums.append(jnp.zeros((size, 1), F32))
                        continue
                    counts = counts_ref[group * GROUP + inner].astype(F32)
                    absorbed = level_ref[start : start + size] - jnp.log(counts - dark_all_ref[start : start + size])
                    absorbed_ref[place : place + size] = absorbed.astype(BF16)
                    sums.append(jnp.sum(absorbed, axis=1, keepdims=True))
            means = jnp.broadcast_to(jnp.concatenate(sums, axis=0) / cols, (GROUP * ext, CELL)).astype(BF16)
            both = jnp.dot(rowband_ref[...], means, preferred_element_type=F32)
            level = (both[:height] + both[height:]).astype(BF16)
            here = slice(group * height, (group + 1) * height)
            held_ref[here, :CELL] = -level
            held_ref[here, CELL + cols :] = -level
            level = jnp.concatenate([level.astype(F32)] * (TILE // CELL), axis=1)
            for at_col in range(0, cols, TILE):
                both = jnp.dot(rowband_ref[...], absorbed_ref[:, at_col : at_col + TILE], preferred_element_type=F32)
                less = both[:height] + both[height:] - level
                held_ref[here, CELL + at_col : CELL + at_col + TILE] = less.astype(BF16)
        total = jnp.zeros((groups * height, 1), F32)
        for at_col in range(0, cols, TILE):
            window = held_ref[:, at_col : at_col + TILE + 2 * CELL]
            piece = jnp.dot(window, colband_ref[0], preferred_element_type=F32) + jnp.dot(
                window, colband_ref[1], preferred_element_type=F32
            )
            at_half = at_col // 2
            smooth_ref[:, at_half : at_half + CELL] = piece[:, :CELL]
            smooth_ref[:, cols // 2 + at_half : cols // 2 + at_half + CELL] = piece[:, CELL:]
            total = total + jnp.sum(piece, axis=1, keepdims=True)
        mean = total / cols
        for group in range(groups):
            for step in range(row_count):
                for up in range(upper):
                    start = group * height + (step * upper + up) * per_block
                    centered = smooth_ref[start : start + per_block] - mean[start : start + per_block]
                    out_refs[step][group, up] = centered.astype(BF16)


def lowpass(place, raw, near, far, dark, flat, rowband, colband, row_count, upper, share, wants_inner, after):
    planes, rows, cols = raw.shape
    ext = rows + 2 * HALO
    groups = planes // GROUP
    shape = jax.ShapeDtypeStruct((groups, upper, GROUP * share, cols), BF16)
    return pl.pallas_call(
        skipping(functools.partial(lowpass_kernel, groups, row_count, upper, share, wants_inner), 8, len(after)),
        out_shape=[shape] * row_count,
        in_specs=[pl.BlockSpec(memory_space=pltpu.SMEM)] + whole(7) + anywhere(len(after)),
        out_specs=whole(row_count),
        scratch_shapes=[
            pltpu.VMEM((ext, cols), F32),
            pltpu.VMEM((ext, cols), F32),
            pltpu.VMEM((GROUP * ext, cols), BF16),
            pltpu.VMEM((planes * rows, cols + 2 * CELL), BF16),
            pltpu.VMEM((planes * rows, cols), F32),
        ],
        compiler_params=call_params(24),
        cost_estimate=cost(6.5),
    )(place, raw, near, far, dark, flat, rowband, colband, *after)


def route_kernel(row_count, ang_count, upper, place_ref, *rest):
    slots, targets, sems = rest[:row_count], rest[row_count:-1], rest[-1]
    me, turn = place_ref[0], place_ref[2]
    for step in range(1, ang_count):
        target = turn ^ step
        slot = me ^ (target // upper)
        for number in range(row_count):

            @pl.when(slot == number)
            def _():
                pltpu.make_async_copy(slots[number].at[:, target % upper], targets[step - 1], sems.at[step]).start()

    for step in range(1, ang_count):
        pltpu.make_async_copy(slots[0].at[:, 0], targets[step - 1], sems.at[step]).wait()


def route(place, slots, ang_count, after):
    groups, upper, lines, cols = slots[0].shape
    return pl.pallas_call(
        skipping(functools.partial(route_kernel, len(slots), ang_count, upper), 1 + len(slots)),
        out_shape=[jax.ShapeDtypeStruct((groups, lines, cols), BF16)] * (ang_count - 1),
        in_specs=[pl.BlockSpec(memory_space=pltpu.SMEM)] + anywhere(len(slots) + 1),
        out_specs=whole(ang_count - 1),
        scratch_shapes=[pltpu.SemaphoreType.DMA((ang_count,))],
        compiler_params=call_params(8),
        cost_estimate=cost(2.0),
    )(place, *slots, after)


def ramp_kernel(cols, to_even_ref, to_odd_ref, weave_ref):
    steps = cols // (2 * TILE)
    for out_ref, parity in ((to_even_ref, 1), (to_odd_ref, -1)):
        for block in range(2 * steps - 1):
            source = lax.broadcasted_iota(jnp.int32, (TILE, TILE), 0) + (block - (steps - 1)) * TILE
            distance = 2 * (source - lax.broadcasted_iota(jnp.int32, (TILE, TILE), 1)) + parity
            spacing = distance.astype(F32)
            falloff = -4.0 / (math.pi * math.pi * (spacing * spacing))
            out_ref[block * TILE : (block + 1) * TILE] = falloff.astype(BF16)
    source = lax.broadcasted_iota(jnp.int32, (TILE, TILE), 0)
    target = lax.broadcasted_iota(jnp.int32, (TILE, TILE), 1)
    place = jnp.where(source < CELL, 2 * source, 2 * (source - CELL) + 1)
    weave_ref[...] = (place == target).astype(F32).astype(BF16)


def ramp_lines(lines, half, to_even_ref, to_odd_ref, weave_ref, store):
    steps = half // TILE
    for block in range(steps):
        rows = slice((steps - 1 - block) * TILE, (steps - 1 - block) * TILE + half)
        here = slice(block * TILE, (block + 1) * TILE)
        there = slice(half + block * TILE, half + (block + 1) * TILE)
        even = lines(here).astype(F32) + jnp.dot(
            lines(slice(half, 2 * half)), to_even_ref[rows], preferred_element_type=F32
        )
        odd = lines(there).astype(F32) + jnp.dot(lines(slice(0, half)), to_odd_ref[rows], preferred_element_type=F32)
        even, odd = even.astype(BF16), odd.astype(BF16)
        for part in range(TILE // CELL):
            span = slice(part * CELL, (part + 1) * CELL)
            both = jnp.concatenate([even[:, span], odd[:, span]], axis=1)
            store(
                (TILE // CELL) * block + part, jnp.dot(both, weave_ref[...], preferred_element_type=F32).astype(BF16)
            )


def correlate(share, slots, lanes, cols, pick_ref, add, lead_ref, mate_ref, ls_ref, ms_ref):
    half, reach = cols // 2, SPAN // 2
    padded, width = half + 2 * reach, CELL + 2 * reach
    picks = share * slots
    for parity in range(2):
        start = parity * padded
        mate_ref[:, start : start + reach] = jnp.zeros((picks, reach), BF16)
        mate_ref[:, start + reach + half : start + padded] = jnp.zeros((picks, reach), BF16)
        for at_col in range(0, half, TILE):
            here = parity * half + at_col
            picked = 0.0
            for lane, lines in enumerate(lanes):
                values = lines(slice(here, here + TILE))
                at = lane * lane_width(values.shape[0])
                ones = pick_ref[:, at : at + values.shape[0]]
                picked = picked + jnp.dot(ones, values, preferred_element_type=F32)
            picked = picked.astype(BF16)
            lead_ref[:, here : here + TILE] = picked[:picks]
            place = start + reach + at_col
            mate_ref[:, place : place + TILE] = picked[picks:]
    cells = half // CELL

    def one_row(row, _):
        span = pl.ds(pl.multiple_of(row * slots, slots), slots)
        for cell in range(cells):
            stack = slice(cell * slots, (cell + 1) * slots)
            back = (cells - 1 - cell) * CELL
            for parity in range(2):
                at = parity * half + cell * CELL
                ls_ref[stack, parity * CELL : (parity + 1) * CELL] = lead_ref[span, at : at + CELL]
                at = parity * padded + back
                ms_ref[stack, parity * width : (parity + 1) * width] = mate_ref[span, at : at + width]
        products = lax.dot_general(ls_ref[...], ms_ref[...], (((0,), (0,)), ((), ())), preferred_element_type=F32)
        tables = (
            products[:CELL, :width],
            products[CELL:, width:],
            products[:CELL, width:] + products[CELL:, :width],
        )
        for number, table in enumerate(tables):
            skewed = pltpu.roll(table, 0, 1, stride=1, stride_axis=0)
            add(row, number, jnp.sum(skewed, axis=0, keepdims=True))
        return 0

    lax.fori_loop(0, share, one_row, 0, unroll=UNROLL)


def select_shifts(profile_ref, shifts, scale, width):
    reach = SPAN // 2
    middle = CELL + reach - 1 - lax.shift_right_arithmetic(shifts, 1)
    odd = (shifts & 1) == 1
    wanted = (jnp.where(odd, middle, -1), jnp.where(odd, middle - 1, -1), jnp.where(odd, -1, middle))
    at = lax.broadcasted_iota(jnp.int32, (width, shifts.shape[1]), 0)
    total = jnp.zeros((profile_ref.shape[0], shifts.shape[1]), F32)
    for number, place in enumerate(wanted):
        selector = (at == place).astype(F32).astype(BF16)
        rest = profile_ref[:, number * width : (number + 1) * width]
        for _ in range(3):
            high = rest.astype(BF16)
            total = total + jnp.dot(high, selector, preferred_element_type=F32)
            rest = rest - high.astype(F32)
    return total * scale


def flat(ref, span, first=None, count=None):
    part = ref[:, :, span] if first is None else ref[first : first + count, :, span]
    return part.reshape(part.shape[0] * part.shape[1], part.shape[2])


def finish_kernel(
    upper, slot_count, ang_count, wants_inner, parts, has_out, has_old, has_other, share, slots, scale, *refs
):
    refs = list(refs)
    take = lambda count: [refs.pop(0) for _ in range(count)]
    late = ang_count - late_lanes(ang_count)
    lanes = ang_count if 1 in parts else late
    last, loads, gives_own = 1 in parts, 0 in parts, parts == (0,)
    place_ref, *ramp_refs = take(4)
    slot_refs, pieces, picks = take(slot_count), take(lanes - 1 if loads else lanes), take(len(parts))
    (shifts_ref,) = take(1) if last else (None,)
    take(1 if has_out else 0)
    (old_ref,) = take(1) if has_old else (None,)
    (other_ref,) = take(1) if has_other else (None,)
    out_ref, result_ref = take(2)
    (own_ref,) = take(1) if gives_own else (None,)
    (x_ref,) = take(1) if loads else (None,)
    y_ref, in_sems, out_sems, profile_ref = take(4)
    me, turn = place_ref[0], place_ref[2]
    active = place_ref[3] == wants_inner
    groups, lines_each, cols = pieces[0].shape

    @pl.when(active)
    def _():
        if loads:
            targets = [x_ref.at[:groups]] + ([own_ref] if gives_own else [])
            sems = (in_sems.at[0], in_sems.at[ang_count])
            for number, slot in enumerate(slot_refs):

                @pl.when(me ^ (turn // upper) == number)
                def _():
                    for target, sem in zip(targets, sems):
                        pltpu.make_async_copy(slot.at[:, turn % upper], target, sem).start()

            copies = [pltpu.make_async_copy(slot_refs[0].at[:, 0], target, sem) for target, sem in zip(targets, sems)]
            for lane in range(1, lanes):
                target = x_ref.at[lane * groups : (lane + 1) * groups]
                copies.append(pltpu.make_async_copy(pieces[lane - 1], target, in_sems.at[lane]))
                copies[-1].start()
            for copy in copies:
                copy.wait()
            known = [lambda span, at=lane * groups: flat(x_ref, span, at, groups) for lane in range(lanes)]
        else:
            known = [lambda span, ref=piece: flat(ref, span) for piece in pieces]
        width = CELL + SPAN
        started = []
        for number, part in enumerate(parts):
            low, high = (0, late) if part == 0 else (late, ang_count)

            def lines(span, low=low, high=high):
                if loads:
                    return flat(x_ref, span, low * groups, (high - low) * groups)
                values = [read(span) for read in known[low:high]]
                return values[0] if len(values) == 1 else jnp.concatenate(values, axis=0)

            base = 0 if loads else late

            def store(block, values, low=low - base, high=high - base):
                here = slice(block * TILE, (block + 1) * TILE)
                y_ref[low * groups : high * groups, :, here] = values.reshape((high - low) * groups, lines_each, TILE)

            ramp_lines(lines, cols // 2, *ramp_refs, store)
            for lane in range(low, high):
                target = out_ref.at[pl.ds((turn ^ lane) * groups, groups)]
                source = y_ref.at[(lane - base) * groups : (lane - base + 1) * groups]
                started.append(pltpu.make_async_copy(source, target, out_sems.at[lane]))
                started[-1].start()

            def add(row, table, values, number=number, part=part):
                at = (pl.ds(row, 1), slice(table * width, (table + 1) * width))
                if number:
                    values = values + profile_ref[at]
                elif part:
                    values = values + old_ref[at]
                profile_ref[at] = values

            correlate(share, slots, known[:high], cols, picks[number], add, *refs)
        result_ref[...] = select_shifts(profile_ref, shifts_ref[...], scale, width) if last else profile_ref[...]
        for copy in started:
            copy.wait()

    @pl.when(jnp.logical_not(active))
    def _():
        result_ref[...] = other_ref[...] if has_other else jnp.zeros(result_ref.shape, F32)


def finish(place, ramp, slots, pieces, picks, shifts, out, old, other, wants_inner, parts, upper, share, half, after):
    loads, last, gives_own = 0 in parts, 1 in parts, parts == (0,)
    ang_count = len(pieces) + (1 if loads else 0)
    groups, lines_each, cols = pieces[0].shape
    lanes = ang_count if last else ang_count - late_lanes(ang_count)
    number = pair_slots(half)
    pieces = pieces[: lanes - 1] if loads else pieces
    args = [place, *ramp, *slots, *pieces, *(picks[part] for part in parts)]
    specs = [pl.BlockSpec(memory_space=pltpu.SMEM)] + whole(3)
    specs = specs + (anywhere if loads else whole)(len(slots) + len(pieces)) + whole(len(parts))
    cells, width = cols // (2 * CELL), CELL + SPAN
    if last:
        args, specs = args + [shifts], specs + whole(1)
    aliases = {}
    if out is not None:
        aliases[len(args)] = 0
        args, specs = args + [out], specs + anywhere(1)
    if old is not None:
        args, specs = args + [old], specs + whole(1)
    if other is not None:
        args, specs = args + [other], specs + whole(1)
    args, specs = args + [after], specs + anywhere(1)
    kernel = functools.partial(
        finish_kernel, upper, len(slots), ang_count, wants_inner, parts, out is not None, old is not None,
        other is not None, share, number, (half * cols) ** (-0.5),
    )
    lines = lambda count: (groups * count, lines_each, cols)
    return pl.pallas_call(
        skipping(kernel, len(args) - 1),
        out_shape=[
            jax.ShapeDtypeStruct(lines(ang_count), BF16),
            jax.ShapeDtypeStruct((share, shifts.shape[1] if last else 3 * width), F32),
        ]
        + [jax.ShapeDtypeStruct(lines(1), BF16)] * gives_own,
        in_specs=specs,
        out_specs=anywhere(1) + whole(1 + gives_own),
        scratch_shapes=[pltpu.VMEM(lines(lanes), BF16)] * loads
        + [
            pltpu.VMEM(lines(lanes if loads else late_lanes(ang_count)), BF16),
            pltpu.SemaphoreType.DMA((ang_count + 1,)),
            pltpu.SemaphoreType.DMA((ang_count,)),
            pltpu.VMEM((share, 3 * width), F32),
            pltpu.VMEM((share * number, cols), BF16),
            pltpu.VMEM((share * number, cols + 2 * SPAN), BF16),
            pltpu.VMEM((cells * number, 2 * CELL), BF16),
            pltpu.VMEM((cells * number, 2 * width), BF16),
        ],
        input_output_aliases=aliases,
        compiler_params=call_params(),
        cost_estimate=cost(5.0 * len(parts)),
    )(*args)


def shards(raw_frames, dark_field, flat_field, kernel_taps, partner, shifts):
    planes, rows, cols = raw_frames.shape
    tap_count = kernel_taps.shape[0]
    half = partner.shape[0]
    row_count, ang_count = lax.axis_size("row"), lax.axis_size("ang")
    upper, share = ang_count // row_count, rows // ang_count
    me, turn = lax.axis_index("row"), lax.axis_index("ang")
    is_inner = lambda at: jnp.logical_and(at > 0, at < row_count - 1).astype(jnp.int32)
    place = jnp.stack([me, is_inner(me), turn, is_inner(turn // upper)]).astype(jnp.int32)

    cross = [(i, i + 1) for i in range(1, row_count - 1, 2)]
    near, far = edges(place, raw_frames, dark_field, flat_field)
    far = lax.ppermute(far, "row", cross + [(j, i) for i, j in cross])
    near = lax.ppermute(near, "row", [(i, i ^ 1) for i in range(row_count)])
    ext = rows + 2 * HALO
    rowband, colband = pl.pallas_call(
        functools.partial(band_kernel, tap_count, rows, row_count, upper, share),
        out_shape=[
            jax.ShapeDtypeStruct((2 * GROUP * rows, GROUP * ext), BF16),
            jax.ShapeDtypeStruct((2, TILE + 2 * CELL, TILE), BF16),
        ],
        in_specs=[pl.BlockSpec(memory_space=pltpu.SMEM)] * 2,
        out_specs=whole(2),
        compiler_params=call_params(),
        cost_estimate=cost(2.0),
    )(place, kernel_taps)
    ramp = pl.pallas_call(
        functools.partial(ramp_kernel, cols),
        out_shape=[jax.ShapeDtypeStruct((cols - TILE, TILE), BF16)] * 2 + [jax.ShapeDtypeStruct((TILE, TILE), BF16)],
        out_specs=whole(3),
        compiler_params=call_params(),
        cost_estimate=cost(1.8),
    )()

    number, late = pair_slots(half), late_lanes(ang_count)

    per_lane = lane_width(planes * share)
    picks = pl.pallas_call(
        functools.partial(pick_kernel, planes, half, number, share),
        out_shape=[
            jax.ShapeDtypeStruct((2 * share * number, lanes * per_lane), BF16) for lanes in (ang_count - late, ang_count)
        ],
        in_specs=[pl.BlockSpec(memory_space=pltpu.SMEM)] * 2,
        out_specs=whole(2),
        compiler_params=call_params(),
        cost_estimate=cost(1.5),
    )(place, partner)
    shifts = shifts[None, :]

    ends = (0, row_count - 1)
    mine = lambda inner, source: (source in ends) != bool(inner)

    def filter_rows(inner, after):
        sent = lowpass(
            place, raw_frames, near, far if inner else near, dark_field, flat_field, rowband, colband,
            row_count, upper, share, inner, after,
        )
        slots = [sent[0]]
        for step in range(1, row_count):
            pairs = [(i, i ^ step) for i in range(row_count) if mine(inner, i)]
            slots.append(lax.ppermute(sent[step], "row", pairs))
        return slots

    def regroup(inner, slots, after):
        pieces = list(route(place, slots, ang_count, after))
        for step in range(1, ang_count):
            pairs = [(i, i ^ step) for i in range(ang_count) if mine(inner, (i ^ step) // upper)]
            pieces[step - 1] = lax.ppermute(pieces[step - 1], "ang", pairs)
        return pieces

    outer = filter_rows(0, [])
    inner = filter_rows(1, [outer[0], ramp[0], picks[0]])
    outer_lines = regroup(0, outer, inner[0])
    inner_lines = regroup(1, inner, inner[0])
    ending = functools.partial(finish, place, ramp)
    out, ends_corr = ending(
        outer, outer_lines, picks, shifts, None, None, None, 0, (0, 1), upper, share, half, inner[0]
    )
    out, profile, own = ending(
        inner, inner_lines, picks, shifts, out, None, None, 1, (0,), upper, share, half, ends_corr
    )
    filtered, correlation = ending(
        [], [own, *inner_lines], picks, shifts, out, profile, ends_corr, 1, (1,), upper, share, half, profile
    )
    return filtered.reshape(-1, share, cols), correlation


def solution(mesh):
    in_specs = (
        P(("scan", "ang"), "row", None),
        P("row", None),
        P("row", None),
        P(),
        P("scan"),
        P(),
    )
    out_specs = (P("scan", ("ang", "row"), None), P(("scan", "ang", "row"), None))
    return jax.shard_map(shards, mesh=mesh, in_specs=in_specs, out_specs=out_specs, check_vma=False)
```

```python
import functools
import math

import jax
import jax.numpy as jnp
from jax import lax
from jax.experimental import pallas as pl
from jax.experimental.pallas import tpu as pltpu
from jax.sharding import PartitionSpec as P

SPAN = 256
HALO = 16
GROUP = 4
TILE = 256
CELL = 128
UNROLL = 2

F32 = jnp.float32
BF16 = jnp.bfloat16


def call_params(mebibytes=16):
    return pltpu.CompilerParams(vmem_limit_bytes=mebibytes << 20)


def whole(count):
    return [pl.BlockSpec(memory_space=pltpu.VMEM)] * count


def anywhere(count):
    return [pl.BlockSpec(memory_space=pl.ANY)] * count


def cost(micros):
    return pl.CostEstimate(flops=int(micros * 1.15e9), bytes_accessed=1 << 16, transcendentals=0)


def skipping(kernel, at, count=1):
    return lambda *refs: kernel(*refs[:at], *refs[at + count :])


def split_hi_lo(values):
    high = values.astype(BF16)
    return high, (values - high.astype(F32)).astype(BF16)


def banded(index, taps_ref, tap_count):
    total = jnp.zeros(index.shape, F32)
    for tap in range(tap_count):
        total = jnp.where(index == tap, taps_ref[tap], total)
    return total


def late_lanes(ang_count):
    return max(1, ang_count // 4)


def lane_width(lines):
    return -(-lines // CELL) * CELL


def pair_slots(half):
    return -(-(half // 2 + 1) // 16) * 16


def pick_kernel(planes, half, slots, share, place_ref, partner_ref, *pick_refs):
    turn = place_ref[2]
    picks = share * slots
    pick_at = lax.broadcasted_iota(jnp.int32, (picks, 1), 0)
    row, first = pick_at // slots, pick_at % slots
    lanes_early = pick_refs[0].shape[1]
    leads = [jnp.full((picks, 1), -1, jnp.int32) for _ in pick_refs]
    mates = list(leads)
    counts = [jnp.int32(0) for _ in pick_refs]

    def stands(plane):
        return (turn ^ (plane // planes)) * lane_width(planes * share) + plane % planes * share

    for plane in range(half):
        lead, mate = stands(plane), stands(partner_ref[plane])
        late = jnp.maximum(lead, mate) >= lanes_early
        for part, mine in enumerate((jnp.logical_not(late), late)):
            here = first == jnp.where(mine, counts[part], -1)
            leads[part] = jnp.where(here, lead + row, leads[part])
            mates[part] = jnp.where(here, mate + row, mates[part])
            counts[part] = counts[part] + jnp.where(mine, 1, 0)
    for part, pick_ref in enumerate(pick_refs):
        line_at = lax.broadcasted_iota(jnp.int32, (picks, pick_ref.shape[1]), 1)
        pick_ref[:picks] = (line_at == leads[part]).astype(F32).astype(BF16)
        pick_ref[picks:] = (line_at == mates[part]).astype(F32).astype(BF16)


def band_kernel(
    tap_count, rows, row_count, upper, share, place_ref, taps_ref, rowband_ref, farband_ref, colband_ref
):
    me = place_ref[0]
    odd = lax.rem(me, 2)
    margin = tap_count // 2
    height = GROUP * rows
    for out_ref, depth, skip in ((rowband_ref, rows + 2 * HALO, 0), (farband_ref, HALO, rows + HALO)):
        out_at = lax.broadcasted_iota(jnp.int32, (height, GROUP * depth), 0)
        in_at = lax.broadcasted_iota(jnp.int32, (height, GROUP * depth), 1)
        line = out_at % share
        plane = (out_at // share) % GROUP
        block = out_at // (share * GROUP)
        step, up = block // upper, block % upper
        row = (up * row_count + (step ^ me)) * share + line
        place = in_at % depth + skip
        straight = place - HALO
        crossed = jnp.where(place < HALO, rows + place, jnp.where(place >= rows + HALO, place - rows - 2 * HALO, straight))
        source = jnp.where(odd == 1, straight, crossed)
        index = jnp.where(in_at // depth == plane, source - row + margin, -1)
        high, low = split_hi_lo(banded(index, taps_ref, tap_count))
        out_ref[:height] = high
        out_ref[height:] = low
    width = TILE + 2 * CELL
    from_at = lax.broadcasted_iota(jnp.int32, (width, TILE), 0)
    lane = lax.broadcasted_iota(jnp.int32, (width, TILE), 1)
    to_at = jnp.where(lane < CELL, 2 * lane, 2 * (lane - CELL) + 1)
    high, low = split_hi_lo(banded(from_at - CELL - to_at + margin, taps_ref, tap_count))
    colband_ref[0] = high
    colband_ref[1] = low


def edge_kernel(planes, rows, place_ref, raw_ref, dark_ref, flat_ref, near_ref, far_ref, held_ref, in_sems, out_sems):
    odd = lax.rem(place_ref[0], 2)
    near_at = pl.multiple_of((1 - odd) * (rows - HALO), HALO)
    far_at = pl.multiple_of(odd * (rows - HALO), HALO)
    loads, stores = [], []
    for side, (out_ref, start) in enumerate(((far_ref, far_at), (near_ref, near_at))):
        span, held = pl.ds(start, HALO), held_ref.at[side]
        loads.append(
            [
                pltpu.make_async_copy(raw_ref.at[:, span], held.at[:planes], in_sems.at[side, 0]),
                pltpu.make_async_copy(dark_ref.at[span], held.at[planes], in_sems.at[side, 1]),
                pltpu.make_async_copy(flat_ref.at[span], held.at[planes + 1], in_sems.at[side, 2]),
            ]
        )
        stores.append(pltpu.make_async_copy(held, out_ref, out_sems.at[side]))
    for side in loads:
        for copy in side:
            copy.start()
    for side, store in zip(loads, stores):
        for copy in side:
            copy.wait()
        store.start()
    for store in stores:
        store.wait()


def edges(place, raw, dark, flat):
    planes, rows, cols = raw.shape
    return pl.pallas_call(
        functools.partial(edge_kernel, planes, rows),
        out_shape=[jax.ShapeDtypeStruct((planes + 2, HALO, cols), BF16)] * 2,
        in_specs=[pl.BlockSpec(memory_space=pltpu.SMEM)] + anywhere(3),
        out_specs=anywhere(2),
        scratch_shapes=[
            pltpu.VMEM((2, planes + 2, HALO, cols), BF16),
            pltpu.SemaphoreType.DMA((2, 3)),
            pltpu.SemaphoreType.DMA((2,)),
        ],
        compiler_params=call_params(60),
        cost_estimate=cost(2.0),
    )(place, raw, dark, flat)


def free_steps(rows, row_count, upper, share, margin):
    def reached(me, step):
        for up in range(upper):
            start = (up * row_count + (me ^ step)) * share
            if start + share - 1 + margin >= rows if me % 2 else start < margin:
                return True
        return False

    count = 0
    while count < row_count and not any(reached(me, count) for me in range(1, row_count - 1)):
        count += 1
    return count


def smooth_lines(groups, upper, share, steps, height, row_dot, colband_ref, held_ref, smooth_ref, out_refs):
    cols = smooth_ref.shape[1]
    per_block = GROUP * share
    low, high = steps[0] * upper * per_block, (steps[-1] + 1) * upper * per_block
    count = high - low
    for group in range(groups):
        here = slice(group * count, (group + 1) * count)
        level = row_dot(group, None, low, high).astype(BF16)
        held_ref[here, :CELL] = -level
        held_ref[here, CELL + cols :] = -level
        level = jnp.concatenate([level.astype(F32)] * (TILE // CELL), axis=1)
        for at_col in range(0, cols, TILE):
            less = row_dot(group, slice(at_col, at_col + TILE), low, high) - level
            held_ref[here, CELL + at_col : CELL + at_col + TILE] = less.astype(BF16)
    lines = slice(0, groups * count)
    total = jnp.zeros((groups * count, 1), F32)
    for at_col in range(0, cols, TILE):
        window = held_ref[lines, at_col : at_col + TILE + 2 * CELL]
        piece = jnp.dot(window, colband_ref[0], preferred_element_type=F32) + jnp.dot(
            window, colband_ref[1], preferred_element_type=F32
        )
        at_half = at_col // 2
        smooth_ref[lines, at_half : at_half + CELL] = piece[:, :CELL]
        smooth_ref[lines, cols // 2 + at_half : cols // 2 + at_half + CELL] = piece[:, CELL:]
        total = total + jnp.sum(piece, axis=1, keepdims=True)
    mean = total / cols
    for group in range(groups):
        for number, step in enumerate(steps):
            for up in range(upper):
                start = group * count + (number * upper + up) * per_block
                centered = smooth_ref[start : start + per_block] - mean[start : start + per_block]
                out_refs[step][group, up] = centered.astype(BF16)


def band_rows(band_ref, values, height, low, high):
    if high - low == height:
        both = jnp.dot(band_ref[...], values, preferred_element_type=F32)
    else:
        rows = jnp.concatenate([band_ref[low:high], band_ref[height + low : height + high]], axis=0)
        both = jnp.dot(rows, values, preferred_element_type=F32)
    return both[: high - low] + both[high - low :]


def near_kernel(
    groups, row_count, upper, share, free,
    place_ref, raw_ref, near_ref, dark_ref, flat_ref, rowband_ref, colband_ref, *rest
):
    out_refs, (absorbed_ref, means_ref, level_ref, dark_all_ref, held_ref, smooth_ref) = rest[:row_count], rest[row_count:]
    planes, rows, cols = raw_ref.shape
    ext, height = rows + 2 * HALO, GROUP * rows
    spans = ((0, HALO), (HALO, rows))
    fields = ((near_ref[planes], near_ref[planes + 1]), (dark_ref[...], flat_ref[...]))
    for (start, size), (darkness, brightness) in zip(spans, fields):
        darkness = darkness.astype(F32)
        dark_all_ref[start : start + size] = darkness
        level_ref[start : start + size] = jnp.log(brightness.astype(F32) - darkness)
    for plane in range(planes):
        for (start, size), counts_ref in zip(spans, (near_ref, raw_ref)):
            place = slice(plane * ext + start, plane * ext + start + size)
            counts = counts_ref[plane].astype(F32)
            absorbed = level_ref[start : start + size] - jnp.log(counts - dark_all_ref[start : start + size])
            absorbed_ref[place] = absorbed.astype(BF16)
            mean = jnp.sum(absorbed, axis=1, keepdims=True) / cols
            means_ref[place] = jnp.broadcast_to(mean, (size, CELL)).astype(BF16)
        place = slice(plane * ext + HALO + rows, (plane + 1) * ext)
        absorbed_ref[place] = jnp.zeros((HALO, cols), BF16)
        means_ref[place] = jnp.zeros((HALO, CELL), BF16)

    def row_dot(group, span, low, high):
        here = slice(group * GROUP * ext, (group + 1) * GROUP * ext)
        values = means_ref[here] if span is None else absorbed_ref[here, span]
        return band_rows(rowband_ref, values, height, low, high)

    for inner, steps in ((0, range(row_count)), (1, range(free))):
        if steps:

            @pl.when(place_ref[1] == inner)
            def _():
                smooth_lines(
                    groups, upper, share, steps, height, row_dot, colband_ref, held_ref, smooth_ref, out_refs
                )


def far_kernel(
    groups, row_count, upper, share, free,
    place_ref, far_ref, absorbed_ref, means_ref, rowband_ref, farband_ref, colband_ref, *rest
):
    out_refs, (far_absorbed_ref, far_means_ref, held_ref, smooth_ref) = rest[: row_count - free], rest[row_count - free :]
    planes, cols = far_ref.shape[0] - 2, far_ref.shape[2]
    rows = absorbed_ref.shape[0] // planes - 2 * HALO
    ext, height = rows + 2 * HALO, GROUP * rows

    @pl.when(place_ref[1] == 1)
    def _():
        darkness = far_ref[planes].astype(F32)
        level = jnp.log(far_ref[planes + 1].astype(F32) - darkness)
        for plane in range(planes):
            absorbed = level - jnp.log(far_ref[plane].astype(F32) - darkness)
            place = slice(plane * HALO, (plane + 1) * HALO)
            far_absorbed_ref[place] = absorbed.astype(BF16)
            mean = jnp.sum(absorbed, axis=1, keepdims=True) / cols
            far_means_ref[place] = jnp.broadcast_to(mean, (HALO, CELL)).astype(BF16)

        def row_dot(group, span, low, high):
            here = slice(group * GROUP * ext, (group + 1) * GROUP * ext)
            there = slice(group * GROUP * HALO, (group + 1) * GROUP * HALO)
            values = means_ref[here] if span is None else absorbed_ref[here, span]
            others = far_means_ref[there] if span is None else far_absorbed_ref[there, span]
            return band_rows(rowband_ref, values, height, low, high) + band_rows(farband_ref, others, height, low, high)

        smooth_lines(
            groups, upper, share, range(free, row_count), height, row_dot, colband_ref, held_ref, smooth_ref,
            [None] * free + list(out_refs),
        )


def lowpass_call(kernel, free, place, inputs, planes, rows, cols, row_count, upper, share, outs, extra, scratch, micros, after):
    groups = planes // GROUP
    shape = jax.ShapeDtypeStruct((groups, upper, GROUP * share, cols), BF16)
    return pl.pallas_call(
        skipping(functools.partial(kernel, groups, row_count, upper, share, free), 1 + len(inputs), len(after)),
        out_shape=[shape] * outs + extra,
        in_specs=[pl.BlockSpec(memory_space=pltpu.SMEM)] + whole(len(inputs)) + anywhere(len(after)),
        out_specs=whole(outs + len(extra)),
        scratch_shapes=scratch
        + [pltpu.VMEM((planes * rows, cols + 2 * CELL), BF16), pltpu.VMEM((planes * rows, cols), F32)],
        compiler_params=call_params(24),
        cost_estimate=cost(micros),
    )(place, *inputs, *after)


def route_kernel(row_count, ang_count, upper, place_ref, *rest):
    slots, targets, sems = rest[:row_count], rest[row_count:-1], rest[-1]
    me, turn = place_ref[0], place_ref[2]
    for step in range(1, ang_count):
        target = turn ^ step
        slot = me ^ (target // upper)
        for number in range(row_count):

            @pl.when(slot == number)
            def _():
                pltpu.make_async_copy(slots[number].at[:, target % upper], targets[step - 1], sems.at[step]).start()

    for step in range(1, ang_count):
        pltpu.make_async_copy(slots[0].at[:, 0], targets[step - 1], sems.at[step]).wait()


def route(place, slots, ang_count, after):
    groups, upper, lines, cols = slots[0].shape
    return pl.pallas_call(
        skipping(functools.partial(route_kernel, len(slots), ang_count, upper), 1 + len(slots)),
        out_shape=[jax.ShapeDtypeStruct((groups, lines, cols), BF16)] * (ang_count - 1),
        in_specs=[pl.BlockSpec(memory_space=pltpu.SMEM)] + anywhere(len(slots) + 1),
        out_specs=whole(ang_count - 1),
        scratch_shapes=[pltpu.SemaphoreType.DMA((ang_count,))],
        compiler_params=call_params(8),
        cost_estimate=cost(2.0),
    )(place, *slots, after)


def ramp_kernel(cols, to_even_ref, to_odd_ref, weave_ref):
    steps = cols // (2 * TILE)
    for out_ref, parity in ((to_even_ref, 1), (to_odd_ref, -1)):
        for block in range(2 * steps - 1):
            source = lax.broadcasted_iota(jnp.int32, (TILE, TILE), 0) + (block - (steps - 1)) * TILE
            distance = 2 * (source - lax.broadcasted_iota(jnp.int32, (TILE, TILE), 1)) + parity
            spacing = distance.astype(F32)
            falloff = -4.0 / (math.pi * math.pi * (spacing * spacing))
            out_ref[block * TILE : (block + 1) * TILE] = falloff.astype(BF16)
    source = lax.broadcasted_iota(jnp.int32, (TILE, TILE), 0)
    target = lax.broadcasted_iota(jnp.int32, (TILE, TILE), 1)
    place = jnp.where(source < CELL, 2 * source, 2 * (source - CELL) + 1)
    weave_ref[...] = (place == target).astype(F32).astype(BF16)


def ramp_lines(lines, half, to_even_ref, to_odd_ref, weave_ref, store):
    steps = half // TILE
    for block in range(steps):
        rows = slice((steps - 1 - block) * TILE, (steps - 1 - block) * TILE + half)
        here = slice(block * TILE, (block + 1) * TILE)
        there = slice(half + block * TILE, half + (block + 1) * TILE)
        even = lines(here).astype(F32) + jnp.dot(
            lines(slice(half, 2 * half)), to_even_ref[rows], preferred_element_type=F32
        )
        odd = lines(there).astype(F32) + jnp.dot(lines(slice(0, half)), to_odd_ref[rows], preferred_element_type=F32)
        even, odd = even.astype(BF16), odd.astype(BF16)
        for part in range(TILE // CELL):
            span = slice(part * CELL, (part + 1) * CELL)
            both = jnp.concatenate([even[:, span], odd[:, span]], axis=1)
            store(
                (TILE // CELL) * block + part, jnp.dot(both, weave_ref[...], preferred_element_type=F32).astype(BF16)
            )


def pick_lines(lanes, cols, pick_ref, lead_ref, mate_ref):
    half, reach = cols // 2, SPAN // 2
    padded, picks = half + 2 * reach, lead_ref.shape[0]
    for parity in range(2):
        start = parity * padded
        mate_ref[:, start : start + reach] = jnp.zeros((picks, reach), BF16)
        mate_ref[:, start + reach + half : start + padded] = jnp.zeros((picks, reach), BF16)
        for at_col in range(0, half, TILE):
            here = parity * half + at_col
            picked = 0.0
            for lane, lines in enumerate(lanes):
                values = lines(slice(here, here + TILE))
                at = lane * lane_width(values.shape[0])
                ones = pick_ref[:, at : at + values.shape[0]]
                picked = picked + jnp.dot(ones, values, preferred_element_type=F32)
            picked = picked.astype(BF16)
            lead_ref[:, here : here + TILE] = picked[:picks]
            place = start + reach + at_col
            mate_ref[:, place : place + TILE] = picked[picks:]


def add_lines(lanes, first, are_leads, cols, pick_ref, some_leads_ref, some_mates_ref, lead_ref, mate_ref):
    half, reach = cols // 2, SPAN // 2
    padded, picks = half + 2 * reach, lead_ref.shape[0]
    to_leads = are_leads.astype(F32)
    rows = pl.ds(pl.multiple_of(jnp.where(are_leads, 0, picks), picks), picks)
    mate_ref[...] = some_mates_ref[...]
    for parity in range(2):
        for at_col in range(0, half, TILE):
            here = parity * half + at_col
            picked = 0.0
            for lane, lines in enumerate(lanes):
                values = lines(slice(here, here + TILE))
                at = (first + lane) * lane_width(values.shape[0])
                picked = picked + jnp.dot(pick_ref[rows, at : at + values.shape[0]], values, preferred_element_type=F32)
            span = slice(here, here + TILE)
            lead_ref[:, span] = (some_leads_ref[:, span].astype(F32) + picked * to_leads).astype(BF16)
            place = parity * padded + reach + at_col
            span = slice(place, place + TILE)
            mate_ref[:, span] = (some_mates_ref[:, span].astype(F32) + picked * (1.0 - to_leads)).astype(BF16)


def correlate(share, slots, cols, add, lead_ref, mate_ref, ls_ref, ms_ref):
    half, reach = cols // 2, SPAN // 2
    padded, width = half + 2 * reach, CELL + 2 * reach
    cells = half // CELL

    def one_row(row, _):
        span = pl.ds(pl.multiple_of(row * slots, slots), slots)
        for cell in range(cells):
            stack = slice(cell * slots, (cell + 1) * slots)
            back = (cells - 1 - cell) * CELL
            for parity in range(2):
                at = parity * half + cell * CELL
                ls_ref[stack, parity * CELL : (parity + 1) * CELL] = lead_ref[span, at : at + CELL]
                at = parity * padded + back
                ms_ref[stack, parity * width : (parity + 1) * width] = mate_ref[span, at : at + width]
        products = lax.dot_general(ls_ref[...], ms_ref[...], (((0,), (0,)), ((), ())), preferred_element_type=F32)
        tables = (
            products[:CELL, :width],
            products[CELL:, width:],
            products[:CELL, width:] + products[CELL:, :width],
        )
        for number, table in enumerate(tables):
            skewed = pltpu.roll(table, 0, 1, stride=1, stride_axis=0)
            add(row, number, jnp.sum(skewed, axis=0, keepdims=True))
        return 0

    lax.fori_loop(0, share, one_row, 0, unroll=UNROLL)


def select_shifts(profile_ref, shifts, scale, width):
    reach = SPAN // 2
    middle = CELL + reach - 1 - lax.shift_right_arithmetic(shifts, 1)
    odd = (shifts & 1) == 1
    wanted = (jnp.where(odd, middle, -1), jnp.where(odd, middle - 1, -1), jnp.where(odd, -1, middle))
    at = lax.broadcasted_iota(jnp.int32, (width, shifts.shape[1]), 0)
    total = jnp.zeros((profile_ref.shape[0], shifts.shape[1]), F32)
    for number, place in enumerate(wanted):
        selector = (at == place).astype(F32).astype(BF16)
        rest = profile_ref[:, number * width : (number + 1) * width]
        for _ in range(3):
            high = rest.astype(BF16)
            total = total + jnp.dot(high, selector, preferred_element_type=F32)
            rest = rest - high.astype(F32)
    return total * scale


def flat(ref, span, first=None, count=None):
    part = ref[:, :, span] if first is None else ref[first : first + count, :, span]
    return part.reshape(part.shape[0] * part.shape[1], part.shape[2])


def finish_kernel(
    upper, slot_count, ang_count, wants_inner, parts, has_out, has_old, has_other, share, slots, scale, *refs
):
    refs = list(refs)
    take = lambda count: [refs.pop(0) for _ in range(count)]
    late = ang_count - late_lanes(ang_count)
    lanes = ang_count if 1 in parts else late
    last, loads, gives_own = 1 in parts, 0 in parts, parts == (0,)
    place_ref, *ramp_refs = take(4)
    slot_refs, pieces = take(slot_count), take(lanes - 1 if loads else lanes)
    picks = dict(zip((0, 1) if loads else (1,), take(2 if loads else 1)))
    some_leads_ref, some_mates_ref = take(2) if not loads else (None, None)
    (shifts_ref,) = take(1) if last else (None,)
    take(1 if has_out else 0)
    (old_ref,) = take(1) if has_old else (None,)
    (other_ref,) = take(1) if has_other else (None,)
    out_ref, result_ref = take(2)
    own_ref, leads_out_ref, mates_out_ref = take(3) if gives_own else (None,) * 3
    (x_ref,) = take(1) if loads else (None,)
    y_ref, in_sems, out_sems, profile_ref = take(4)
    me, turn = place_ref[0], place_ref[2]
    active = place_ref[3] == wants_inner
    groups, lines_each, cols = pieces[0].shape

    @pl.when(active)
    def _():
        if loads:
            targets = [x_ref.at[:groups]] + ([own_ref] if gives_own else [])
            sems = (in_sems.at[0], in_sems.at[ang_count])
            for number, slot in enumerate(slot_refs):

                @pl.when(me ^ (turn // upper) == number)
                def _():
                    for target, sem in zip(targets, sems):
                        pltpu.make_async_copy(slot.at[:, turn % upper], target, sem).start()

            copies = [pltpu.make_async_copy(slot_refs[0].at[:, 0], target, sem) for target, sem in zip(targets, sems)]
            for lane in range(1, lanes):
                target = x_ref.at[lane * groups : (lane + 1) * groups]
                copies.append(pltpu.make_async_copy(pieces[lane - 1], target, in_sems.at[lane]))
                copies[-1].start()
            for copy in copies:
                copy.wait()
            known = [lambda span, at=lane * groups: flat(x_ref, span, at, groups) for lane in range(lanes)]
        else:
            known = [lambda span, ref=piece: flat(ref, span) for piece in pieces]
        width = CELL + SPAN
        started = []
        for number, part in enumerate(parts):
            low, high = (0, late) if part == 0 else (late, ang_count)

            def lines(span, low=low, high=high):
                if loads:
                    return flat(x_ref, span, low * groups, (high - low) * groups)
                values = [read(span) for read in known[low:high]]
                return values[0] if len(values) == 1 else jnp.concatenate(values, axis=0)

            base = 0 if loads else late

            def store(block, values, low=low - base, high=high - base):
                here = slice(block * TILE, (block + 1) * TILE)
                y_ref[low * groups : high * groups, :, here] = values.reshape((high - low) * groups, lines_each, TILE)

            ramp_lines(lines, cols // 2, *ramp_refs, store)
            for lane in range(low, high):
                target = out_ref.at[pl.ds((turn ^ lane) * groups, groups)]
                source = y_ref.at[(lane - base) * groups : (lane - base + 1) * groups]
                started.append(pltpu.make_async_copy(source, target, out_sems.at[lane]))
                started[-1].start()

            def add(row, table, values, number=number, part=part):
                at = (pl.ds(row, 1), slice(table * width, (table + 1) * width))
                if number:
                    values = values + profile_ref[at]
                elif part:
                    values = values + old_ref[at]
                profile_ref[at] = values

            lead_ref, mate_ref, *stacks = refs
            if loads:
                pick_lines(known[:high], cols, picks[part], lead_ref, mate_ref)
            else:
                are_leads = (turn ^ late) < ang_count // 2
                add_lines(
                    known[late:], late, are_leads, cols, picks[1], some_leads_ref, some_mates_ref, lead_ref, mate_ref
                )
            correlate(share, slots, cols, add, lead_ref, mate_ref, *stacks)
        if gives_own:
            pick_lines(known, cols, picks[1], leads_out_ref, mates_out_ref)
        result_ref[...] = select_shifts(profile_ref, shifts_ref[...], scale, width) if last else profile_ref[...]
        for copy in started:
            copy.wait()

    @pl.when(jnp.logical_not(active))
    def _():
        result_ref[...] = other_ref[...] if has_other else jnp.zeros(result_ref.shape, F32)


def finish(place, ramp, slots, pieces, picks, some, shifts, out, old, other, wants_inner, parts, upper, share, half, after):
    loads, last, gives_own = 0 in parts, 1 in parts, parts == (0,)
    ang_count = len(pieces) + (1 if loads else 0)
    groups, lines_each, cols = pieces[0].shape
    lanes = ang_count if last else ang_count - late_lanes(ang_count)
    number = pair_slots(half)
    pieces = pieces[: lanes - 1] if loads else pieces
    args = [place, *ramp, *slots, *pieces, *(picks if loads else picks[1:]), *some]
    specs = [pl.BlockSpec(memory_space=pltpu.SMEM)] + whole(3)
    specs = specs + (anywhere if loads else whole)(len(slots) + len(pieces)) + whole(2 if loads else 1 + len(some))
    cells, width = cols // (2 * CELL), CELL + SPAN
    if last:
        args, specs = args + [shifts], specs + whole(1)
    aliases = {}
    if out is not None:
        aliases[len(args)] = 0
        args, specs = args + [out], specs + anywhere(1)
    if old is not None:
        args, specs = args + [old], specs + whole(1)
    if other is not None:
        args, specs = args + [other], specs + whole(1)
    args, specs = args + [after], specs + anywhere(1)
    kernel = functools.partial(
        finish_kernel, upper, len(slots), ang_count, wants_inner, parts, out is not None, old is not None,
        other is not None, share, number, (half * cols) ** (-0.5),
    )
    lines = lambda count: (groups * count, lines_each, cols)
    return pl.pallas_call(
        skipping(kernel, len(args) - 1),
        out_shape=[
            jax.ShapeDtypeStruct(lines(ang_count), BF16),
            jax.ShapeDtypeStruct((share, shifts.shape[1] if last else 3 * width), F32),
        ]
        + [
            jax.ShapeDtypeStruct(lines(1), BF16),
            jax.ShapeDtypeStruct((share * number, cols), BF16),
            jax.ShapeDtypeStruct((share * number, cols + 2 * SPAN), BF16),
        ]
        * gives_own,
        in_specs=specs,
        out_specs=anywhere(1) + whole(1 + 3 * gives_own),
        scratch_shapes=[pltpu.VMEM(lines(lanes), BF16)] * loads
        + [
            pltpu.VMEM(lines(lanes if loads else late_lanes(ang_count)), BF16),
            pltpu.SemaphoreType.DMA((ang_count + 1,)),
            pltpu.SemaphoreType.DMA((ang_count,)),
            pltpu.VMEM((share, 3 * width), F32),
            pltpu.VMEM((share * number, cols), BF16),
            pltpu.VMEM((share * number, cols + 2 * SPAN), BF16),
            pltpu.VMEM((cells * number, 2 * CELL), BF16),
            pltpu.VMEM((cells * number, 2 * width), BF16),
        ],
        input_output_aliases=aliases,
        compiler_params=call_params(),
        cost_estimate=cost(5.0 * len(parts)),
    )(*args)


def shards(raw_frames, dark_field, flat_field, kernel_taps, partner, shifts):
    planes, rows, cols = raw_frames.shape
    tap_count = kernel_taps.shape[0]
    half = partner.shape[0]
    row_count, ang_count = lax.axis_size("row"), lax.axis_size("ang")
    upper, share = ang_count // row_count, rows // ang_count
    me, turn = lax.axis_index("row"), lax.axis_index("ang")
    is_inner = lambda at: jnp.logical_and(at > 0, at < row_count - 1).astype(jnp.int32)
    place = jnp.stack([me, is_inner(me), turn, is_inner(turn // upper)]).astype(jnp.int32)

    cross = [(i, i + 1) for i in range(1, row_count - 1, 2)]
    near, far = edges(place, raw_frames, dark_field, flat_field)
    far = lax.ppermute(far, "row", cross + [(j, i) for i, j in cross])
    near = lax.ppermute(near, "row", [(i, i ^ 1) for i in range(row_count)])
    ext = rows + 2 * HALO
    rowband, farband, colband = pl.pallas_call(
        functools.partial(band_kernel, tap_count, rows, row_count, upper, share),
        out_shape=[
            jax.ShapeDtypeStruct((2 * GROUP * rows, GROUP * ext), BF16),
            jax.ShapeDtypeStruct((2 * GROUP * rows, GROUP * HALO), BF16),
            jax.ShapeDtypeStruct((2, TILE + 2 * CELL, TILE), BF16),
        ],
        in_specs=[pl.BlockSpec(memory_space=pltpu.SMEM)] * 2,
        out_specs=whole(3),
        compiler_params=call_params(),
        cost_estimate=cost(2.0),
    )(place, kernel_taps)
    ramp = pl.pallas_call(
        functools.partial(ramp_kernel, cols),
        out_shape=[jax.ShapeDtypeStruct((cols - TILE, TILE), BF16)] * 2 + [jax.ShapeDtypeStruct((TILE, TILE), BF16)],
        out_specs=whole(3),
        compiler_params=call_params(),
        cost_estimate=cost(1.8),
    )()

    number, late = pair_slots(half), late_lanes(ang_count)

    per_lane = lane_width(planes * share)
    picks = pl.pallas_call(
        functools.partial(pick_kernel, planes, half, number, share),
        out_shape=[
            jax.ShapeDtypeStruct((2 * share * number, lanes * per_lane), BF16) for lanes in (ang_count - late, ang_count)
        ],
        in_specs=[pl.BlockSpec(memory_space=pltpu.SMEM)] * 2,
        out_specs=whole(2),
        compiler_params=call_params(),
        cost_estimate=cost(1.5),
    )(place, partner)
    shifts = shifts[None, :]

    ends = (0, row_count - 1)
    mine = lambda inner, source: (source in ends) != bool(inner)

    free = free_steps(rows, row_count, upper, share, tap_count // 2)
    sizes = (planes, rows, cols, row_count, upper, share)
    *begun, absorbed, means = lowpass_call(
        near_kernel, free, place, [raw_frames, near, dark_field, flat_field, rowband, colband], *sizes, row_count,
        [jax.ShapeDtypeStruct((planes * ext, cols), BF16), jax.ShapeDtypeStruct((planes * ext, CELL), BF16)],
        [pltpu.VMEM((rows + HALO, cols), F32)] * 2, 6.5, [],
    )
    ended = lowpass_call(
        far_kernel, free, place, [far, absorbed, means, rowband, farband, colband], *sizes, row_count - free, [],
        [pltpu.VMEM((planes * HALO, cols), BF16), pltpu.VMEM((planes * HALO, CELL), BF16)], 3.5,
        [begun[0], ramp[0], picks[0]],
    )

    def exchange(step, sent, wanted):
        return lax.ppermute(sent, "row", [(i, i ^ step) for i in range(row_count) if wanted(i)])

    any_row = lambda source: True
    common = [begun[0] if step == 0 else exchange(step, begun[step], any_row) for step in range(free)]
    outer = common + [exchange(step, begun[step], functools.partial(mine, 0)) for step in range(free, row_count)]
    inner = common + [exchange(step, ended[step - free], functools.partial(mine, 1)) for step in range(free, row_count)]
    if not free:
        outer[0], inner[0] = begun[0], ended[0]

    def regroup(inner, slots, after):
        pieces = list(route(place, slots, ang_count, after))
        for step in range(1, ang_count):
            pairs = [(i, i ^ step) for i in range(ang_count) if mine(inner, (i ^ step) // upper)]
            pieces[step - 1] = lax.ppermute(pieces[step - 1], "ang", pairs)
        return pieces

    outer_lines = regroup(0, outer, ended[0])
    inner_lines = regroup(1, inner, ended[0])
    ending = functools.partial(finish, place, ramp)
    out, ends_corr = ending(
        outer, outer_lines, picks, [], shifts, None, None, None, 0, (0, 1), upper, share, half, ended[0]
    )
    out, profile, own, *some = ending(
        inner, inner_lines, picks, [], shifts, out, None, None, 1, (0,), upper, share, half, ends_corr
    )
    filtered, correlation = ending(
        [], [own, *inner_lines], picks, some, shifts, out, profile, ends_corr, 1, (1,), upper, share, half, profile
    )
    return filtered.reshape(-1, share, cols), correlation


def solution(mesh):
    in_specs = (
        P(("scan", "ang"), "row", None),
        P("row", None),
        P("row", None),
        P(),
        P("scan"),
        P(),
    )
    out_specs = (P("scan", ("ang", "row"), None), P(("scan", "ang", "row"), None))
    return jax.shard_map(shards, mesh=mesh, in_specs=in_specs, out_specs=out_specs, check_vma=False)
```

```python
import functools
import math

import jax
import jax.numpy as jnp
from jax import lax
from jax.experimental import pallas as pl
from jax.experimental.pallas import tpu as pltpu
from jax.sharding import PartitionSpec as P

SPAN = 256
HALO = 16
GROUP = 4
TILE = 256
CELL = 128
UNROLL = 2

F32 = jnp.float32
BF16 = jnp.bfloat16


def call_params(mebibytes=16):
    return pltpu.CompilerParams(vmem_limit_bytes=mebibytes << 20)


def whole(count):
    return [pl.BlockSpec(memory_space=pltpu.VMEM)] * count


def anywhere(count):
    return [pl.BlockSpec(memory_space=pl.ANY)] * count


def cost(micros):
    return pl.CostEstimate(flops=int(micros * 1.15e9), bytes_accessed=1 << 16, transcendentals=0)


def skipping(kernel, at, count=1):
    return lambda *refs: kernel(*refs[:at], *refs[at + count :])


def split_hi_lo(values):
    high = values.astype(BF16)
    return high, (values - high.astype(F32)).astype(BF16)


def banded(index, taps_ref, tap_count):
    total = jnp.zeros(index.shape, F32)
    for tap in range(tap_count):
        total = jnp.where(index == tap, taps_ref[tap], total)
    return total


def late_lanes(ang_count):
    return max(1, ang_count // 4)


def lane_width(lines):
    return -(-lines // CELL) * CELL


def pair_slots(half):
    return -(-(half // 2 + 1) // 16) * 16


def pick_kernel(planes, half, slots, share, place_ref, partner_ref, *pick_refs):
    turn = place_ref[2]
    picks = share * slots
    pick_at = lax.broadcasted_iota(jnp.int32, (picks, 1), 0)
    row, first = pick_at // slots, pick_at % slots
    lanes_early = pick_refs[0].shape[1]
    leads = [jnp.full((picks, 1), -1, jnp.int32) for _ in pick_refs]
    mates = list(leads)
    counts = [jnp.int32(0) for _ in pick_refs]

    def stands(plane):
        return (turn ^ (plane // planes)) * lane_width(planes * share) + plane % planes * share

    for plane in range(half):
        lead, mate = stands(plane), stands(partner_ref[plane])
        late = jnp.maximum(lead, mate) >= lanes_early
        for part, mine in enumerate((jnp.logical_not(late), late)):
            here = first == jnp.where(mine, counts[part], -1)
            leads[part] = jnp.where(here, lead + row, leads[part])
            mates[part] = jnp.where(here, mate + row, mates[part])
            counts[part] = counts[part] + jnp.where(mine, 1, 0)
    for part, pick_ref in enumerate(pick_refs):
        line_at = lax.broadcasted_iota(jnp.int32, (picks, pick_ref.shape[1]), 1)
        pick_ref[:picks] = (line_at == leads[part]).astype(F32).astype(BF16)
        pick_ref[picks:] = (line_at == mates[part]).astype(F32).astype(BF16)


def band_kernel(
    tap_count, rows, row_count, upper, share, place_ref, taps_ref, rowband_ref, farband_ref, colband_ref
):
    me = place_ref[0]
    odd = lax.rem(me, 2)
    margin = tap_count // 2
    height = GROUP * rows
    for out_ref, depth, skip in ((rowband_ref, rows + 2 * HALO, 0), (farband_ref, HALO, rows + HALO)):
        out_at = lax.broadcasted_iota(jnp.int32, (height, GROUP * depth), 0)
        in_at = lax.broadcasted_iota(jnp.int32, (height, GROUP * depth), 1)
        line = out_at % share
        plane = (out_at // share) % GROUP
        block = out_at // (share * GROUP)
        step, up = block // upper, block % upper
        row = (up * row_count + (step ^ me)) * share + line
        place = in_at % depth + skip
        straight = place - HALO
        crossed = jnp.where(place < HALO, rows + place, jnp.where(place >= rows + HALO, place - rows - 2 * HALO, straight))
        source = jnp.where(odd == 1, straight, crossed)
        index = jnp.where(in_at // depth == plane, source - row + margin, -1)
        high, low = split_hi_lo(banded(index, taps_ref, tap_count))
        out_ref[:height] = high
        out_ref[height:] = low
    width = TILE + 2 * CELL
    from_at = lax.broadcasted_iota(jnp.int32, (width, TILE), 0)
    lane = lax.broadcasted_iota(jnp.int32, (width, TILE), 1)
    to_at = jnp.where(lane < CELL, 2 * lane, 2 * (lane - CELL) + 1)
    high, low = split_hi_lo(banded(from_at - CELL - to_at + margin, taps_ref, tap_count))
    colband_ref[0] = high
    colband_ref[1] = low


def edge_kernel(planes, rows, place_ref, raw_ref, dark_ref, flat_ref, near_ref, far_ref, held_ref, in_sems, out_sems):
    odd = lax.rem(place_ref[0], 2)
    near_at = pl.multiple_of((1 - odd) * (rows - HALO), HALO)
    far_at = pl.multiple_of(odd * (rows - HALO), HALO)
    loads, stores = [], []
    for side, (out_ref, start) in enumerate(((far_ref, far_at), (near_ref, near_at))):
        span, held = pl.ds(start, HALO), held_ref.at[side]
        loads.append(
            [
                pltpu.make_async_copy(raw_ref.at[:, span], held.at[:planes], in_sems.at[side, 0]),
                pltpu.make_async_copy(dark_ref.at[span], held.at[planes], in_sems.at[side, 1]),
                pltpu.make_async_copy(flat_ref.at[span], held.at[planes + 1], in_sems.at[side, 2]),
            ]
        )
        stores.append(pltpu.make_async_copy(held, out_ref, out_sems.at[side]))
    for side in loads:
        for copy in side:
            copy.start()
    for side, store in zip(loads, stores):
        for copy in side:
            copy.wait()
        store.start()
    for store in stores:
        store.wait()


def edges(place, raw, dark, flat):
    planes, rows, cols = raw.shape
    return pl.pallas_call(
        functools.partial(edge_kernel, planes, rows),
        out_shape=[jax.ShapeDtypeStruct((planes + 2, HALO, cols), BF16)] * 2,
        in_specs=[pl.BlockSpec(memory_space=pltpu.SMEM)] + anywhere(3),
        out_specs=anywhere(2),
        scratch_shapes=[
            pltpu.VMEM((2, planes + 2, HALO, cols), BF16),
            pltpu.SemaphoreType.DMA((2, 3)),
            pltpu.SemaphoreType.DMA((2,)),
        ],
        compiler_params=call_params(60),
        cost_estimate=cost(2.0),
    )(place, raw, dark, flat)


def free_steps(rows, row_count, upper, share, margin):
    def reached(me, step):
        for up in range(upper):
            start = (up * row_count + (me ^ step)) * share
            if start + share - 1 + margin >= rows if me % 2 else start < margin:
                return True
        return False

    count = 0
    while count < row_count and not any(reached(me, count) for me in range(1, row_count - 1)):
        count += 1
    return count


def smooth_lines(groups, upper, share, steps, height, row_dot, colband_ref, held_ref, smooth_ref, out_refs):
    cols = smooth_ref.shape[1]
    per_block = GROUP * share
    low, high = steps[0] * upper * per_block, (steps[-1] + 1) * upper * per_block
    count = high - low
    for group in range(groups):
        here = slice(group * count, (group + 1) * count)
        level = row_dot(group, None, low, high).astype(BF16)
        held_ref[here, :CELL] = -level
        held_ref[here, CELL + cols :] = -level
        level = jnp.concatenate([level.astype(F32)] * (TILE // CELL), axis=1)
        for at_col in range(0, cols, TILE):
            less = row_dot(group, slice(at_col, at_col + TILE), low, high) - level
            held_ref[here, CELL + at_col : CELL + at_col + TILE] = less.astype(BF16)
    lines = slice(0, groups * count)
    total = jnp.zeros((groups * count, 1), F32)
    for at_col in range(0, cols, TILE):
        window = held_ref[lines, at_col : at_col + TILE + 2 * CELL]
        piece = jnp.dot(window, colband_ref[0], preferred_element_type=F32) + jnp.dot(
            window, colband_ref[1], preferred_element_type=F32
        )
        at_half = at_col // 2
        smooth_ref[lines, at_half : at_half + CELL] = piece[:, :CELL]
        smooth_ref[lines, cols // 2 + at_half : cols // 2 + at_half + CELL] = piece[:, CELL:]
        total = total + jnp.sum(piece, axis=1, keepdims=True)
    mean = total / cols
    for group in range(groups):
        for number, step in enumerate(steps):
            for up in range(upper):
                start = group * count + (number * upper + up) * per_block
                centered = smooth_ref[start : start + per_block] - mean[start : start + per_block]
                out_refs[step][group, up] = centered.astype(BF16)


def band_rows(band_ref, values, height, low, high):
    if high - low == height:
        both = jnp.dot(band_ref[...], values, preferred_element_type=F32)
    else:
        rows = jnp.concatenate([band_ref[low:high], band_ref[height + low : height + high]], axis=0)
        both = jnp.dot(rows, values, preferred_element_type=F32)
    return both[: high - low] + both[high - low :]


def near_kernel(
    groups, row_count, upper, share, free,
    place_ref, raw_ref, near_ref, dark_ref, flat_ref, rowband_ref, colband_ref, *rest
):
    out_refs, (absorbed_ref, means_ref, level_ref, dark_all_ref, held_ref, smooth_ref) = rest[:row_count], rest[row_count:]
    planes, rows, cols = raw_ref.shape
    ext, height = rows + 2 * HALO, GROUP * rows
    spans = ((0, HALO), (HALO, rows))
    fields = ((near_ref[planes], near_ref[planes + 1]), (dark_ref[...], flat_ref[...]))
    for (start, size), (darkness, brightness) in zip(spans, fields):
        darkness = darkness.astype(F32)
        dark_all_ref[start : start + size] = darkness
        level_ref[start : start + size] = jnp.log(brightness.astype(F32) - darkness)
    for plane in range(planes):
        for (start, size), counts_ref in zip(spans, (near_ref, raw_ref)):
            place = slice(plane * ext + start, plane * ext + start + size)
            counts = counts_ref[plane].astype(F32)
            absorbed = level_ref[start : start + size] - jnp.log(counts - dark_all_ref[start : start + size])
            absorbed_ref[place] = absorbed.astype(BF16)
            mean = jnp.sum(absorbed, axis=1, keepdims=True) / cols
            means_ref[place] = jnp.broadcast_to(mean, (size, CELL)).astype(BF16)
        place = slice(plane * ext + HALO + rows, (plane + 1) * ext)
        absorbed_ref[place] = jnp.zeros((HALO, cols), BF16)
        means_ref[place] = jnp.zeros((HALO, CELL), BF16)

    def row_dot(group, span, low, high):
        here = slice(group * GROUP * ext, (group + 1) * GROUP * ext)
        values = means_ref[here] if span is None else absorbed_ref[here, span]
        return band_rows(rowband_ref, values, height, low, high)

    for inner, steps in ((0, range(row_count)), (1, range(free))):
        if steps:

            @pl.when(place_ref[1] == inner)
            def _():
                smooth_lines(
                    groups, upper, share, steps, height, row_dot, colband_ref, held_ref, smooth_ref, out_refs
                )


def far_kernel(
    groups, row_count, upper, share, free,
    place_ref, far_ref, absorbed_ref, means_ref, rowband_ref, farband_ref, colband_ref, *rest
):
    out_refs, (far_absorbed_ref, far_means_ref, held_ref, smooth_ref) = rest[: row_count - free], rest[row_count - free :]
    planes, cols = far_ref.shape[0] - 2, far_ref.shape[2]
    rows = absorbed_ref.shape[0] // planes - 2 * HALO
    ext, height = rows + 2 * HALO, GROUP * rows

    @pl.when(place_ref[1] == 1)
    def _():
        darkness = far_ref[planes].astype(F32)
        level = jnp.log(far_ref[planes + 1].astype(F32) - darkness)
        for plane in range(planes):
            absorbed = level - jnp.log(far_ref[plane].astype(F32) - darkness)
            place = slice(plane * HALO, (plane + 1) * HALO)
            far_absorbed_ref[place] = absorbed.astype(BF16)
            mean = jnp.sum(absorbed, axis=1, keepdims=True) / cols
            far_means_ref[place] = jnp.broadcast_to(mean, (HALO, CELL)).astype(BF16)

        def row_dot(group, span, low, high):
            here = slice(group * GROUP * ext, (group + 1) * GROUP * ext)
            there = slice(group * GROUP * HALO, (group + 1) * GROUP * HALO)
            values = means_ref[here] if span is None else absorbed_ref[here, span]
            others = far_means_ref[there] if span is None else far_absorbed_ref[there, span]
            return band_rows(rowband_ref, values, height, low, high) + band_rows(farband_ref, others, height, low, high)

        smooth_lines(
            groups, upper, share, range(free, row_count), height, row_dot, colband_ref, held_ref, smooth_ref,
            [None] * free + list(out_refs),
        )


def lowpass_call(kernel, free, place, inputs, planes, rows, cols, row_count, upper, share, outs, extra, scratch, micros, after):
    groups = planes // GROUP
    shape = jax.ShapeDtypeStruct((groups, upper, GROUP * share, cols), BF16)
    return pl.pallas_call(
        skipping(functools.partial(kernel, groups, row_count, upper, share, free), 1 + len(inputs), len(after)),
        out_shape=[shape] * outs + extra,
        in_specs=[pl.BlockSpec(memory_space=pltpu.SMEM)] + whole(len(inputs)) + anywhere(len(after)),
        out_specs=whole(outs + len(extra)),
        scratch_shapes=scratch
        + [pltpu.VMEM((planes * rows, cols + 2 * CELL), BF16), pltpu.VMEM((planes * rows, cols), F32)],
        compiler_params=call_params(24),
        cost_estimate=cost(micros),
    )(place, *inputs, *after)


def route_kernel(row_count, upper, steps, sets, place_ref, *rest):
    held, (targets, sems) = rest[: sets * row_count], (rest[sets * row_count : -1], rest[-1])
    me, turn = place_ref[0], place_ref[2]
    for at, (step, wanted) in enumerate(steps):
        target = turn ^ step
        owner = target // upper
        inner = jnp.logical_and(owner > 0, owner < row_count - 1).astype(jnp.int32)
        first = inner * row_count if wanted is None else wanted * row_count
        for number, slot_ref in enumerate(held):

            @pl.when(first + (me ^ owner) == number)
            def _():
                pltpu.make_async_copy(slot_ref.at[:, target % upper], targets[at], sems.at[at]).start()

    for at in range(len(steps)):
        pltpu.make_async_copy(held[0].at[:, 0], targets[at], sems.at[at]).wait()


def route(place, sets, steps, upper, after):
    row_count = len(sets[0])
    groups, _, lines, cols = sets[0][0].shape
    slots = [slot for held in sets for slot in held]
    return pl.pallas_call(
        skipping(functools.partial(route_kernel, row_count, upper, steps, len(sets)), 1 + len(slots)),
        out_shape=[jax.ShapeDtypeStruct((groups, lines, cols), BF16)] * len(steps),
        in_specs=[pl.BlockSpec(memory_space=pltpu.SMEM)] + anywhere(len(slots) + 1),
        out_specs=whole(len(steps)),
        scratch_shapes=[pltpu.SemaphoreType.DMA((len(steps),))],
        compiler_params=call_params(8),
        cost_estimate=cost(2.0),
    )(place, *slots, after)


def ramp_kernel(cols, to_even_ref, to_odd_ref, weave_ref):
    steps = cols // (2 * TILE)
    for out_ref, parity in ((to_even_ref, 1), (to_odd_ref, -1)):
        for block in range(2 * steps - 1):
            source = lax.broadcasted_iota(jnp.int32, (TILE, TILE), 0) + (block - (steps - 1)) * TILE
            distance = 2 * (source - lax.broadcasted_iota(jnp.int32, (TILE, TILE), 1)) + parity
            spacing = distance.astype(F32)
            falloff = -4.0 / (math.pi * math.pi * (spacing * spacing))
            out_ref[block * TILE : (block + 1) * TILE] = falloff.astype(BF16)
    source = lax.broadcasted_iota(jnp.int32, (TILE, TILE), 0)
    target = lax.broadcasted_iota(jnp.int32, (TILE, TILE), 1)
    place = jnp.where(source < CELL, 2 * source, 2 * (source - CELL) + 1)
    weave_ref[...] = (place == target).astype(F32).astype(BF16)


def ramp_lines(lines, half, to_even_ref, to_odd_ref, weave_ref, store):
    steps = half // TILE
    for block in range(steps):
        rows = slice((steps - 1 - block) * TILE, (steps - 1 - block) * TILE + half)
        here = slice(block * TILE, (block + 1) * TILE)
        there = slice(half + block * TILE, half + (block + 1) * TILE)
        even = lines(here).astype(F32) + jnp.dot(
            lines(slice(half, 2 * half)), to_even_ref[rows], preferred_element_type=F32
        )
        odd = lines(there).astype(F32) + jnp.dot(lines(slice(0, half)), to_odd_ref[rows], preferred_element_type=F32)
        even, odd = even.astype(BF16), odd.astype(BF16)
        for part in range(TILE // CELL):
            span = slice(part * CELL, (part + 1) * CELL)
            both = jnp.concatenate([even[:, span], odd[:, span]], axis=1)
            store(
                (TILE // CELL) * block + part, jnp.dot(both, weave_ref[...], preferred_element_type=F32).astype(BF16)
            )


def pick_lines(lanes, cols, pick_ref, lead_ref, mate_ref):
    half, reach = cols // 2, SPAN // 2
    padded, picks = half + 2 * reach, lead_ref.shape[0]
    for parity in range(2):
        start = parity * padded
        mate_ref[:, start : start + reach] = jnp.zeros((picks, reach), BF16)
        mate_ref[:, start + reach + half : start + padded] = jnp.zeros((picks, reach), BF16)
        for at_col in range(0, half, TILE):
            here = parity * half + at_col
            picked = 0.0
            for lane, lines in enumerate(lanes):
                values = lines(slice(here, here + TILE))
                at = lane * lane_width(values.shape[0])
                ones = pick_ref[:, at : at + values.shape[0]]
                picked = picked + jnp.dot(ones, values, preferred_element_type=F32)
            picked = picked.astype(BF16)
            lead_ref[:, here : here + TILE] = picked[:picks]
            place = start + reach + at_col
            mate_ref[:, place : place + TILE] = picked[picks:]


def add_lines(lanes, first, are_leads, cols, pick_ref, some_leads_ref, some_mates_ref, lead_ref, mate_ref):
    half, reach = cols // 2, SPAN // 2
    padded, picks = half + 2 * reach, lead_ref.shape[0]
    to_leads = are_leads.astype(F32)
    rows = pl.ds(pl.multiple_of(jnp.where(are_leads, 0, picks), picks), picks)
    mate_ref[...] = some_mates_ref[...]
    for parity in range(2):
        for at_col in range(0, half, TILE):
            here = parity * half + at_col
            picked = 0.0
            for lane, lines in enumerate(lanes):
                values = lines(slice(here, here + TILE))
                at = (first + lane) * lane_width(values.shape[0])
                picked = picked + jnp.dot(pick_ref[rows, at : at + values.shape[0]], values, preferred_element_type=F32)
            span = slice(here, here + TILE)
            lead_ref[:, span] = (some_leads_ref[:, span].astype(F32) + picked * to_leads).astype(BF16)
            place = parity * padded + reach + at_col
            span = slice(place, place + TILE)
            mate_ref[:, span] = (some_mates_ref[:, span].astype(F32) + picked * (1.0 - to_leads)).astype(BF16)


def correlate(share, slots, cols, add, lead_ref, mate_ref, ls_ref, ms_ref):
    half, reach = cols // 2, SPAN // 2
    padded, width = half + 2 * reach, CELL + 2 * reach
    cells = half // CELL

    def one_row(row, _):
        span = pl.ds(pl.multiple_of(row * slots, slots), slots)
        for cell in range(cells):
            stack = slice(cell * slots, (cell + 1) * slots)
            back = (cells - 1 - cell) * CELL
            for parity in range(2):
                at = parity * half + cell * CELL
                ls_ref[stack, parity * CELL : (parity + 1) * CELL] = lead_ref[span, at : at + CELL]
                at = parity * padded + back
                ms_ref[stack, parity * width : (parity + 1) * width] = mate_ref[span, at : at + width]
        products = lax.dot_general(ls_ref[...], ms_ref[...], (((0,), (0,)), ((), ())), preferred_element_type=F32)
        tables = (
            products[:CELL, :width],
            products[CELL:, width:],
            products[:CELL, width:] + products[CELL:, :width],
        )
        for number, table in enumerate(tables):
            skewed = pltpu.roll(table, 0, 1, stride=1, stride_axis=0)
            add(row, number, jnp.sum(skewed, axis=0, keepdims=True))
        return 0

    lax.fori_loop(0, share, one_row, 0, unroll=UNROLL)


def select_shifts(profile_ref, shifts, scale, width):
    reach = SPAN // 2
    middle = CELL + reach - 1 - lax.shift_right_arithmetic(shifts, 1)
    odd = (shifts & 1) == 1
    wanted = (jnp.where(odd, middle, -1), jnp.where(odd, middle - 1, -1), jnp.where(odd, -1, middle))
    at = lax.broadcasted_iota(jnp.int32, (width, shifts.shape[1]), 0)
    total = jnp.zeros((profile_ref.shape[0], shifts.shape[1]), F32)
    for number, place in enumerate(wanted):
        selector = (at == place).astype(F32).astype(BF16)
        rest = profile_ref[:, number * width : (number + 1) * width]
        for _ in range(3):
            high = rest.astype(BF16)
            total = total + jnp.dot(high, selector, preferred_element_type=F32)
            rest = rest - high.astype(F32)
    return total * scale


def flat(ref, span, first=None, count=None):
    part = ref[:, :, span] if first is None else ref[first : first + count, :, span]
    return part.reshape(part.shape[0] * part.shape[1], part.shape[2])


def finish_kernel(
    upper, slot_count, ang_count, wants_inner, parts, has_out, has_old, has_other, share, slots, scale, *refs
):
    refs = list(refs)
    take = lambda count: [refs.pop(0) for _ in range(count)]
    late = ang_count - late_lanes(ang_count)
    lanes = ang_count if 1 in parts else late
    last, loads, gives_own = 1 in parts, 0 in parts, parts == (0,)
    place_ref, *ramp_refs = take(4)
    slot_refs, pieces = take(slot_count), take(lanes - 1 if loads else lanes)
    picks = dict(zip((0, 1) if loads else (1,), take(2 if loads else 1)))
    some_leads_ref, some_mates_ref = take(2) if not loads else (None, None)
    (shifts_ref,) = take(1) if last else (None,)
    take(1 if has_out else 0)
    (old_ref,) = take(1) if has_old else (None,)
    (other_ref,) = take(1) if has_other else (None,)
    out_ref, result_ref = take(2)
    own_ref, leads_out_ref, mates_out_ref = take(3) if gives_own else (None,) * 3
    (x_ref,) = take(1) if loads else (None,)
    y_ref, in_sems, out_sems, profile_ref = take(4)
    me, turn = place_ref[0], place_ref[2]
    active = place_ref[3] == wants_inner
    groups, lines_each, cols = pieces[0].shape

    @pl.when(active)
    def _():
        if loads:
            targets = [x_ref.at[:groups]] + ([own_ref] if gives_own else [])
            sems = (in_sems.at[0], in_sems.at[ang_count])
            for number, slot in enumerate(slot_refs):

                @pl.when(me ^ (turn // upper) == number)
                def _():
                    for target, sem in zip(targets, sems):
                        pltpu.make_async_copy(slot.at[:, turn % upper], target, sem).start()

            copies = [pltpu.make_async_copy(slot_refs[0].at[:, 0], target, sem) for target, sem in zip(targets, sems)]
            for lane in range(1, lanes):
                target = x_ref.at[lane * groups : (lane + 1) * groups]
                copies.append(pltpu.make_async_copy(pieces[lane - 1], target, in_sems.at[lane]))
                copies[-1].start()
            for copy in copies:
                copy.wait()
            known = [lambda span, at=lane * groups: flat(x_ref, span, at, groups) for lane in range(lanes)]
        else:
            known = [lambda span, ref=piece: flat(ref, span) for piece in pieces]
        width = CELL + SPAN
        started = []
        for number, part in enumerate(parts):
            low, high = (0, late) if part == 0 else (late, ang_count)

            def lines(span, low=low, high=high):
                if loads:
                    return flat(x_ref, span, low * groups, (high - low) * groups)
                values = [read(span) for read in known[low:high]]
                return values[0] if len(values) == 1 else jnp.concatenate(values, axis=0)

            base = 0 if loads else late

            def store(block, values, low=low - base, high=high - base):
                here = slice(block * TILE, (block + 1) * TILE)
                y_ref[low * groups : high * groups, :, here] = values.reshape((high - low) * groups, lines_each, TILE)

            ramp_lines(lines, cols // 2, *ramp_refs, store)
            for lane in range(low, high):
                target = out_ref.at[pl.ds((turn ^ lane) * groups, groups)]
                source = y_ref.at[(lane - base) * groups : (lane - base + 1) * groups]
                started.append(pltpu.make_async_copy(source, target, out_sems.at[lane]))
                started[-1].start()

            def add(row, table, values, number=number, part=part):
                at = (pl.ds(row, 1), slice(table * width, (table + 1) * width))
                if number:
                    values = values + profile_ref[at]
                elif part:
                    values = values + old_ref[at]
                profile_ref[at] = values

            lead_ref, mate_ref, *stacks = refs
            if loads:
                pick_lines(known[:high], cols, picks[part], lead_ref, mate_ref)
            else:
                are_leads = (turn ^ late) < ang_count // 2
                add_lines(
                    known[late:], late, are_leads, cols, picks[1], some_leads_ref, some_mates_ref, lead_ref, mate_ref
                )
            correlate(share, slots, cols, add, lead_ref, mate_ref, *stacks)
        if gives_own:
            pick_lines(known, cols, picks[1], leads_out_ref, mates_out_ref)
        result_ref[...] = select_shifts(profile_ref, shifts_ref[...], scale, width) if last else profile_ref[...]
        for copy in started:
            copy.wait()

    @pl.when(jnp.logical_not(active))
    def _():
        result_ref[...] = other_ref[...] if has_other else jnp.zeros(result_ref.shape, F32)


def finish(place, ramp, slots, pieces, picks, some, shifts, out, old, other, wants_inner, parts, upper, share, half, after):
    loads, last, gives_own = 0 in parts, 1 in parts, parts == (0,)
    ang_count = len(pieces) + (1 if loads else 0)
    groups, lines_each, cols = pieces[0].shape
    lanes = ang_count if last else ang_count - late_lanes(ang_count)
    number = pair_slots(half)
    pieces = pieces[: lanes - 1] if loads else pieces
    args = [place, *ramp, *slots, *pieces, *(picks if loads else picks[1:]), *some]
    specs = [pl.BlockSpec(memory_space=pltpu.SMEM)] + whole(3)
    specs = specs + (anywhere if loads else whole)(len(slots) + len(pieces)) + whole(2 if loads else 1 + len(some))
    cells, width = cols // (2 * CELL), CELL + SPAN
    if last:
        args, specs = args + [shifts], specs + whole(1)
    aliases = {}
    if out is not None:
        aliases[len(args)] = 0
        args, specs = args + [out], specs + anywhere(1)
    if old is not None:
        args, specs = args + [old], specs + whole(1)
    if other is not None:
        args, specs = args + [other], specs + whole(1)
    args, specs = args + [after], specs + anywhere(1)
    kernel = functools.partial(
        finish_kernel, upper, len(slots), ang_count, wants_inner, parts, out is not None, old is not None,
        other is not None, share, number, (half * cols) ** (-0.5),
    )
    lines = lambda count: (groups * count, lines_each, cols)
    return pl.pallas_call(
        skipping(kernel, len(args) - 1),
        out_shape=[
            jax.ShapeDtypeStruct(lines(ang_count), BF16),
            jax.ShapeDtypeStruct((share, shifts.shape[1] if last else 3 * width), F32),
        ]
        + [
            jax.ShapeDtypeStruct(lines(1), BF16),
            jax.ShapeDtypeStruct((share * number, cols), BF16),
            jax.ShapeDtypeStruct((share * number, cols + 2 * SPAN), BF16),
        ]
        * gives_own,
        in_specs=specs,
        out_specs=anywhere(1) + whole(1 + 3 * gives_own),
        scratch_shapes=[pltpu.VMEM(lines(lanes), BF16)] * loads
        + [
            pltpu.VMEM(lines(lanes if loads else late_lanes(ang_count)), BF16),
            pltpu.SemaphoreType.DMA((ang_count + 1,)),
            pltpu.SemaphoreType.DMA((ang_count,)),
            pltpu.VMEM((share, 3 * width), F32),
            pltpu.VMEM((share * number, cols), BF16),
            pltpu.VMEM((share * number, cols + 2 * SPAN), BF16),
            pltpu.VMEM((cells * number, 2 * CELL), BF16),
            pltpu.VMEM((cells * number, 2 * width), BF16),
        ],
        input_output_aliases=aliases,
        compiler_params=call_params(),
        cost_estimate=cost(5.0 * len(parts)),
    )(*args)


def shards(raw_frames, dark_field, flat_field, kernel_taps, partner, shifts):
    planes, rows, cols = raw_frames.shape
    tap_count = kernel_taps.shape[0]
    half = partner.shape[0]
    row_count, ang_count = lax.axis_size("row"), lax.axis_size("ang")
    upper, share = ang_count // row_count, rows // ang_count
    me, turn = lax.axis_index("row"), lax.axis_index("ang")
    is_inner = lambda at: jnp.logical_and(at > 0, at < row_count - 1).astype(jnp.int32)
    place = jnp.stack([me, is_inner(me), turn, is_inner(turn // upper)]).astype(jnp.int32)

    cross = [(i, i + 1) for i in range(1, row_count - 1, 2)]
    near, far = edges(place, raw_frames, dark_field, flat_field)
    far = lax.ppermute(far, "row", cross + [(j, i) for i, j in cross])
    near = lax.ppermute(near, "row", [(i, i ^ 1) for i in range(row_count)])
    ext = rows + 2 * HALO
    rowband, farband, colband = pl.pallas_call(
        functools.partial(band_kernel, tap_count, rows, row_count, upper, share),
        out_shape=[
            jax.ShapeDtypeStruct((2 * GROUP * rows, GROUP * ext), BF16),
            jax.ShapeDtypeStruct((2 * GROUP * rows, GROUP * HALO), BF16),
            jax.ShapeDtypeStruct((2, TILE + 2 * CELL, TILE), BF16),
        ],
        in_specs=[pl.BlockSpec(memory_space=pltpu.SMEM)] * 2,
        out_specs=whole(3),
        compiler_params=call_params(),
        cost_estimate=cost(2.0),
    )(place, kernel_taps)
    ramp = pl.pallas_call(
        functools.partial(ramp_kernel, cols),
        out_shape=[jax.ShapeDtypeStruct((cols - TILE, TILE), BF16)] * 2 + [jax.ShapeDtypeStruct((TILE, TILE), BF16)],
        out_specs=whole(3),
        compiler_params=call_params(),
        cost_estimate=cost(1.8),
    )()

    number, late = pair_slots(half), late_lanes(ang_count)

    per_lane = lane_width(planes * share)
    picks = pl.pallas_call(
        functools.partial(pick_kernel, planes, half, number, share),
        out_shape=[
            jax.ShapeDtypeStruct((2 * share * number, lanes * per_lane), BF16) for lanes in (ang_count - late, ang_count)
        ],
        in_specs=[pl.BlockSpec(memory_space=pltpu.SMEM)] * 2,
        out_specs=whole(2),
        compiler_params=call_params(),
        cost_estimate=cost(1.5),
    )(place, partner)
    shifts = shifts[None, :]

    ends = (0, row_count - 1)
    mine = lambda inner, source: (source in ends) != bool(inner)

    free = free_steps(rows, row_count, upper, share, tap_count // 2)
    sizes = (planes, rows, cols, row_count, upper, share)
    *begun, absorbed, means = lowpass_call(
        near_kernel, free, place, [raw_frames, near, dark_field, flat_field, rowband, colband], *sizes, row_count,
        [jax.ShapeDtypeStruct((planes * ext, cols), BF16), jax.ShapeDtypeStruct((planes * ext, CELL), BF16)],
        [pltpu.VMEM((rows + HALO, cols), F32)] * 2, 6.5, [],
    )
    ended = lowpass_call(
        far_kernel, free, place, [far, absorbed, means, rowband, farband, colband], *sizes, row_count - free, [],
        [pltpu.VMEM((planes * HALO, cols), BF16), pltpu.VMEM((planes * HALO, CELL), BF16)], 3.5,
        [begun[0], ramp[0], picks[0]],
    )

    def exchange(step, sent, wanted):
        return lax.ppermute(sent, "row", [(i, i ^ step) for i in range(row_count) if wanted(i)])

    any_row = lambda source: True
    common = [begun[0] if step == 0 else exchange(step, begun[step], any_row) for step in range(free)]
    outer = common + [exchange(step, begun[step], functools.partial(mine, 0)) for step in range(free, row_count)]
    inner = common + [exchange(step, ended[step - free], functools.partial(mine, 1)) for step in range(free, row_count)]
    if not free:
        outer[0], inner[0] = begun[0], ended[0]

    def send(step, lines, wanted):
        pairs = [(i, i ^ step) for i in range(ang_count) if wanted((i ^ step) // upper)]
        return lax.ppermute(lines, "ang", pairs)

    short, long = range(1, ang_count // 2), range(max(1, ang_count // 2), ang_count)
    routed = route(place, [outer], [(step, 0) for step in long], upper, ended[0])
    outer_long = [send(step, lines, functools.partial(mine, 0)) for step, lines in zip(long, routed)]
    steps = [(step, 1) for step in long] + [(step, None) for step in short]
    routed = route(place, [outer, inner], steps, upper, ended[0])
    shared = [send(step, lines, any_row) for step, lines in zip(short, routed[len(long) :])]
    inner_long = [send(step, lines, functools.partial(mine, 1)) for step, lines in zip(long, routed)]
    outer_lines, inner_lines = shared + outer_long, shared + inner_long
    ending = functools.partial(finish, place, ramp)
    out, ends_corr = ending(
        outer, outer_lines, picks, [], shifts, None, None, None, 0, (0, 1), upper, share, half, ended[0]
    )
    out, profile, own, *some = ending(
        inner, inner_lines, picks, [], shifts, out, None, None, 1, (0,), upper, share, half, ends_corr
    )
    filtered, correlation = ending(
        [], [own, *inner_lines], picks, some, shifts, out, profile, ends_corr, 1, (1,), upper, share, half, profile
    )
    return filtered.reshape(-1, share, cols), correlation


def solution(mesh):
    in_specs = (
        P(("scan", "ang"), "row", None),
        P("row", None),
        P("row", None),
        P(),
        P("scan"),
        P(),
    )
    out_specs = (P("scan", ("ang", "row"), None), P(("scan", "ang", "row"), None))
    return jax.shard_map(shards, mesh=mesh, in_specs=in_specs, out_specs=out_specs, check_vma=False)
```

```python
import functools
import math

import jax
import jax.numpy as jnp
from jax import lax
from jax.experimental import pallas as pl
from jax.experimental.pallas import tpu as pltpu
from jax.sharding import PartitionSpec as P

SPAN = 256
HALO = 16
GROUP = 4
TILE = 256
CELL = 128
UNROLL = 2

F32 = jnp.float32
BF16 = jnp.bfloat16


def call_params(mebibytes=16):
    return pltpu.CompilerParams(vmem_limit_bytes=mebibytes << 20)


def whole(count):
    return [pl.BlockSpec(memory_space=pltpu.VMEM)] * count


def anywhere(count):
    return [pl.BlockSpec(memory_space=pl.ANY)] * count


def cost(micros):
    return pl.CostEstimate(flops=int(micros * 1.15e9), bytes_accessed=1 << 16, transcendentals=0)


def skipping(kernel, at, count=1):
    return lambda *refs: kernel(*refs[:at], *refs[at + count :])


def split_hi_lo(values):
    high = values.astype(BF16)
    return high, (values - high.astype(F32)).astype(BF16)


def banded(index, taps_ref, tap_count):
    total = jnp.zeros(index.shape, F32)
    for tap in range(tap_count):
        total = jnp.where(index == tap, taps_ref[tap], total)
    return total


def late_lanes(ang_count):
    return max(1, ang_count // 4)


def lane_width(lines):
    return -(-lines // CELL) * CELL


def pair_slots(half):
    return -(-(half // 2 + 1) // 16) * 16


def pick_kernel(planes, half, slots, share, place_ref, partner_ref, *pick_refs):
    turn = place_ref[2]
    picks = share * slots
    pick_at = lax.broadcasted_iota(jnp.int32, (picks, 1), 0)
    row, first = pick_at // slots, pick_at % slots
    lanes_early = pick_refs[0].shape[1]
    leads = [jnp.full((picks, 1), -1, jnp.int32) for _ in pick_refs]
    mates = list(leads)
    counts = [jnp.int32(0) for _ in pick_refs]

    def stands(plane):
        return (turn ^ (plane // planes)) * lane_width(planes * share) + plane % planes * share

    for plane in range(half):
        lead, mate = stands(plane), stands(partner_ref[plane])
        late = jnp.maximum(lead, mate) >= lanes_early
        for part, mine in enumerate((jnp.logical_not(late), late)):
            here = first == jnp.where(mine, counts[part], -1)
            leads[part] = jnp.where(here, lead + row, leads[part])
            mates[part] = jnp.where(here, mate + row, mates[part])
            counts[part] = counts[part] + jnp.where(mine, 1, 0)
    for part, pick_ref in enumerate(pick_refs):
        line_at = lax.broadcasted_iota(jnp.int32, (picks, pick_ref.shape[1]), 1)
        pick_ref[:picks] = (line_at == leads[part]).astype(F32).astype(BF16)
        pick_ref[picks:] = (line_at == mates[part]).astype(F32).astype(BF16)


def band_kernel(
    tap_count, rows, row_count, upper, share, place_ref, taps_ref, rowband_ref, farband_ref, colband_ref
):
    me = place_ref[0]
    odd = lax.rem(me, 2)
    margin = tap_count // 2
    height = GROUP * rows
    for out_ref, depth, skip in ((rowband_ref, rows + 2 * HALO, 0), (farband_ref, HALO, rows + HALO)):
        out_at = lax.broadcasted_iota(jnp.int32, (height, GROUP * depth), 0)
        in_at = lax.broadcasted_iota(jnp.int32, (height, GROUP * depth), 1)
        line = out_at % share
        plane = (out_at // share) % GROUP
        block = out_at // (share * GROUP)
        step, up = block // upper, block % upper
        row = (up * row_count + (step ^ me)) * share + line
        place = in_at % depth + skip
        straight = place - HALO
        crossed = jnp.where(place < HALO, rows + place, jnp.where(place >= rows + HALO, place - rows - 2 * HALO, straight))
        source = jnp.where(odd == 1, straight, crossed)
        index = jnp.where(in_at // depth == plane, source - row + margin, -1)
        high, low = split_hi_lo(banded(index, taps_ref, tap_count))
        out_ref[:height] = high
        out_ref[height:] = low
    width = TILE + 2 * CELL
    from_at = lax.broadcasted_iota(jnp.int32, (width, TILE), 0)
    lane = lax.broadcasted_iota(jnp.int32, (width, TILE), 1)
    to_at = jnp.where(lane < CELL, 2 * lane, 2 * (lane - CELL) + 1)
    high, low = split_hi_lo(banded(from_at - CELL - to_at + margin, taps_ref, tap_count))
    colband_ref[0] = high
    colband_ref[1] = low


def edge_kernel(planes, rows, place_ref, raw_ref, dark_ref, flat_ref, near_ref, far_ref, held_ref, in_sems, out_sems):
    odd = lax.rem(place_ref[0], 2)
    near_at = pl.multiple_of((1 - odd) * (rows - HALO), HALO)
    far_at = pl.multiple_of(odd * (rows - HALO), HALO)
    loads, stores = [], []
    for side, (out_ref, start) in enumerate(((far_ref, far_at), (near_ref, near_at))):
        span, held = pl.ds(start, HALO), held_ref.at[side]
        loads.append(
            [
                pltpu.make_async_copy(raw_ref.at[:, span], held.at[:planes], in_sems.at[side, 0]),
                pltpu.make_async_copy(dark_ref.at[span], held.at[planes], in_sems.at[side, 1]),
                pltpu.make_async_copy(flat_ref.at[span], held.at[planes + 1], in_sems.at[side, 2]),
            ]
        )
        stores.append(pltpu.make_async_copy(held, out_ref, out_sems.at[side]))
    for side in loads:
        for copy in side:
            copy.start()
    for side, store in zip(loads, stores):
        for copy in side:
            copy.wait()
        store.start()
    for store in stores:
        store.wait()


def edges(place, raw, dark, flat):
    planes, rows, cols = raw.shape
    return pl.pallas_call(
        functools.partial(edge_kernel, planes, rows),
        out_shape=[jax.ShapeDtypeStruct((planes + 2, HALO, cols), BF16)] * 2,
        in_specs=[pl.BlockSpec(memory_space=pltpu.SMEM)] + anywhere(3),
        out_specs=anywhere(2),
        scratch_shapes=[
            pltpu.VMEM((2, planes + 2, HALO, cols), BF16),
            pltpu.SemaphoreType.DMA((2, 3)),
            pltpu.SemaphoreType.DMA((2,)),
        ],
        compiler_params=call_params(60),
        cost_estimate=cost(2.0),
    )(place, raw, dark, flat)


def free_steps(rows, row_count, upper, share, margin):
    def reached(me, step):
        for up in range(upper):
            start = (up * row_count + (me ^ step)) * share
            if start + share - 1 + margin >= rows if me % 2 else start < margin:
                return True
        return False

    count = 0
    while count < row_count and not any(reached(me, count) for me in range(1, row_count - 1)):
        count += 1
    return count


def smooth_lines(groups, upper, share, steps, height, row_dot, colband_ref, held_ref, smooth_ref, out_refs):
    cols = smooth_ref.shape[1]
    per_block = GROUP * share
    low, high = steps[0] * upper * per_block, (steps[-1] + 1) * upper * per_block
    count = high - low
    for group in range(groups):
        here = slice(group * count, (group + 1) * count)
        level = row_dot(group, None, low, high).astype(BF16)
        held_ref[here, :CELL] = -level
        held_ref[here, CELL + cols :] = -level
        level = jnp.concatenate([level.astype(F32)] * (TILE // CELL), axis=1)
        for at_col in range(0, cols, TILE):
            less = row_dot(group, slice(at_col, at_col + TILE), low, high) - level
            held_ref[here, CELL + at_col : CELL + at_col + TILE] = less.astype(BF16)
    lines = slice(0, groups * count)
    total = jnp.zeros((groups * count, 1), F32)
    for at_col in range(0, cols, TILE):
        window = held_ref[lines, at_col : at_col + TILE + 2 * CELL]
        piece = jnp.dot(window, colband_ref[0], preferred_element_type=F32) + jnp.dot(
            window, colband_ref[1], preferred_element_type=F32
        )
        at_half = at_col // 2
        smooth_ref[lines, at_half : at_half + CELL] = piece[:, :CELL]
        smooth_ref[lines, cols // 2 + at_half : cols // 2 + at_half + CELL] = piece[:, CELL:]
        total = total + jnp.sum(piece, axis=1, keepdims=True)
    mean = total / cols
    for group in range(groups):
        for number, step in enumerate(steps):
            for up in range(upper):
                start = group * count + (number * upper + up) * per_block
                centered = smooth_ref[start : start + per_block] - mean[start : start + per_block]
                out_refs[step][group, up] = centered.astype(BF16)


def band_rows(band_ref, values, height, low, high):
    if high - low == height:
        both = jnp.dot(band_ref[...], values, preferred_element_type=F32)
    else:
        rows = jnp.concatenate([band_ref[low:high], band_ref[height + low : height + high]], axis=0)
        both = jnp.dot(rows, values, preferred_element_type=F32)
    return both[: high - low] + both[high - low :]


def near_kernel(
    groups, row_count, upper, share, free,
    place_ref, raw_ref, near_ref, dark_ref, flat_ref, rowband_ref, colband_ref, *rest
):
    out_refs, (absorbed_ref, means_ref, level_ref, dark_all_ref, held_ref, smooth_ref) = rest[:row_count], rest[row_count:]
    planes, rows, cols = raw_ref.shape
    ext, height = rows + 2 * HALO, GROUP * rows
    spans = ((0, HALO), (HALO, rows))
    fields = ((near_ref[planes], near_ref[planes + 1]), (dark_ref[...], flat_ref[...]))
    for (start, size), (darkness, brightness) in zip(spans, fields):
        darkness = darkness.astype(F32)
        dark_all_ref[start : start + size] = darkness
        level_ref[start : start + size] = jnp.log(brightness.astype(F32) - darkness)
    for plane in range(planes):
        for (start, size), counts_ref in zip(spans, (near_ref, raw_ref)):
            place = slice(plane * ext + start, plane * ext + start + size)
            counts = counts_ref[plane].astype(F32)
            absorbed = level_ref[start : start + size] - jnp.log(counts - dark_all_ref[start : start + size])
            absorbed_ref[place] = absorbed.astype(BF16)
            mean = jnp.sum(absorbed, axis=1, keepdims=True) / cols
            means_ref[place] = jnp.broadcast_to(mean, (size, CELL)).astype(BF16)
        place = slice(plane * ext + HALO + rows, (plane + 1) * ext)
        absorbed_ref[place] = jnp.zeros((HALO, cols), BF16)
        means_ref[place] = jnp.zeros((HALO, CELL), BF16)

    def row_dot(group, span, low, high):
        here = slice(group * GROUP * ext, (group + 1) * GROUP * ext)
        values = means_ref[here] if span is None else absorbed_ref[here, span]
        return band_rows(rowband_ref, values, height, low, high)

    for inner, steps in ((0, range(row_count)), (1, range(free))):
        if steps:

            @pl.when(place_ref[1] == inner)
            def _():
                smooth_lines(
                    groups, upper, share, steps, height, row_dot, colband_ref, held_ref, smooth_ref, out_refs
                )


def far_kernel(
    groups, row_count, upper, share, free,
    place_ref, far_ref, absorbed_ref, means_ref, rowband_ref, farband_ref, colband_ref, *rest
):
    out_refs, (far_absorbed_ref, far_means_ref, held_ref, smooth_ref) = rest[: row_count - free], rest[row_count - free :]
    planes, cols = far_ref.shape[0] - 2, far_ref.shape[2]
    rows = absorbed_ref.shape[0] // planes - 2 * HALO
    ext, height = rows + 2 * HALO, GROUP * rows

    @pl.when(place_ref[1] == 1)
    def _():
        darkness = far_ref[planes].astype(F32)
        level = jnp.log(far_ref[planes + 1].astype(F32) - darkness)
        for plane in range(planes):
            absorbed = level - jnp.log(far_ref[plane].astype(F32) - darkness)
            place = slice(plane * HALO, (plane + 1) * HALO)
            far_absorbed_ref[place] = absorbed.astype(BF16)
            mean = jnp.sum(absorbed, axis=1, keepdims=True) / cols
            far_means_ref[place] = jnp.broadcast_to(mean, (HALO, CELL)).astype(BF16)

        def row_dot(group, span, low, high):
            here = slice(group * GROUP * ext, (group + 1) * GROUP * ext)
            there = slice(group * GROUP * HALO, (group + 1) * GROUP * HALO)
            values = means_ref[here] if span is None else absorbed_ref[here, span]
            others = far_means_ref[there] if span is None else far_absorbed_ref[there, span]
            return band_rows(rowband_ref, values, height, low, high) + band_rows(farband_ref, others, height, low, high)

        smooth_lines(
            groups, upper, share, range(free, row_count), height, row_dot, colband_ref, held_ref, smooth_ref,
            [None] * free + list(out_refs),
        )


def lowpass_call(kernel, free, place, inputs, planes, rows, cols, row_count, upper, share, outs, extra, scratch, micros, after):
    groups = planes // GROUP
    shape = jax.ShapeDtypeStruct((groups, upper, GROUP * share, cols), BF16)
    return pl.pallas_call(
        skipping(functools.partial(kernel, groups, row_count, upper, share, free), 1 + len(inputs), len(after)),
        out_shape=[shape] * outs + extra,
        in_specs=[pl.BlockSpec(memory_space=pltpu.SMEM)] + whole(len(inputs)) + anywhere(len(after)),
        out_specs=whole(outs + len(extra)),
        scratch_shapes=scratch
        + [pltpu.VMEM((planes * rows, cols + 2 * CELL), BF16), pltpu.VMEM((planes * rows, cols), F32)],
        compiler_params=call_params(24),
        cost_estimate=cost(micros),
    )(place, *inputs, *after)


def route_kernel(row_count, upper, steps, sets, place_ref, *rest):
    held, (targets, sems) = rest[: sets * row_count], (rest[sets * row_count : -1], rest[-1])
    me, turn = place_ref[0], place_ref[2]
    for at, (step, wanted) in enumerate(steps):
        target = turn ^ step
        owner = target // upper
        inner = jnp.logical_and(owner > 0, owner < row_count - 1).astype(jnp.int32)
        first = inner * row_count if wanted is None else wanted * row_count
        for number, slot_ref in enumerate(held):

            @pl.when(first + (me ^ owner) == number)
            def _():
                pltpu.make_async_copy(slot_ref.at[:, target % upper], targets[at], sems.at[at]).start()

    for at in range(len(steps)):
        pltpu.make_async_copy(held[0].at[:, 0], targets[at], sems.at[at]).wait()


def route(place, sets, steps, upper, after):
    row_count = len(sets[0])
    groups, _, lines, cols = sets[0][0].shape
    slots = [slot for held in sets for slot in held]
    return pl.pallas_call(
        skipping(functools.partial(route_kernel, row_count, upper, steps, len(sets)), 1 + len(slots)),
        out_shape=[jax.ShapeDtypeStruct((groups, lines, cols), BF16)] * len(steps),
        in_specs=[pl.BlockSpec(memory_space=pltpu.SMEM)] + anywhere(len(slots) + 1),
        out_specs=whole(len(steps)),
        scratch_shapes=[pltpu.SemaphoreType.DMA((len(steps),))],
        compiler_params=call_params(8),
        cost_estimate=cost(2.0),
    )(place, *slots, after)


def ramp_kernel(cols, to_even_ref, to_odd_ref, weave_ref):
    steps = cols // (2 * TILE)
    for out_ref, parity in ((to_even_ref, 1), (to_odd_ref, -1)):
        for block in range(2 * steps - 1):
            source = lax.broadcasted_iota(jnp.int32, (TILE, TILE), 0) + (block - (steps - 1)) * TILE
            distance = 2 * (source - lax.broadcasted_iota(jnp.int32, (TILE, TILE), 1)) + parity
            spacing = distance.astype(F32)
            falloff = -4.0 / (math.pi * math.pi * (spacing * spacing))
            out_ref[block * TILE : (block + 1) * TILE] = falloff.astype(BF16)
    source = lax.broadcasted_iota(jnp.int32, (TILE, TILE), 0)
    target = lax.broadcasted_iota(jnp.int32, (TILE, TILE), 1)
    place = jnp.where(source < CELL, 2 * source, 2 * (source - CELL) + 1)
    weave_ref[...] = (place == target).astype(F32).astype(BF16)


def ramp_lines(lines, half, to_even_ref, to_odd_ref, weave_ref, store):
    steps = half // TILE
    for block in range(steps):
        rows = slice((steps - 1 - block) * TILE, (steps - 1 - block) * TILE + half)
        here = slice(block * TILE, (block + 1) * TILE)
        there = slice(half + block * TILE, half + (block + 1) * TILE)
        even = lines(here).astype(F32) + jnp.dot(
            lines(slice(half, 2 * half)), to_even_ref[rows], preferred_element_type=F32
        )
        odd = lines(there).astype(F32) + jnp.dot(lines(slice(0, half)), to_odd_ref[rows], preferred_element_type=F32)
        even, odd = even.astype(BF16), odd.astype(BF16)
        for part in range(TILE // CELL):
            span = slice(part * CELL, (part + 1) * CELL)
            both = jnp.concatenate([even[:, span], odd[:, span]], axis=1)
            store(
                (TILE // CELL) * block + part, jnp.dot(both, weave_ref[...], preferred_element_type=F32).astype(BF16)
            )


def pick_lines(lanes, cols, pick_ref, lead_ref, mate_ref):
    half, reach = cols // 2, SPAN // 2
    padded, picks = half + 2 * reach, lead_ref.shape[0]
    for parity in range(2):
        start = parity * padded
        mate_ref[:, start : start + reach] = jnp.zeros((picks, reach), BF16)
        mate_ref[:, start + reach + half : start + padded] = jnp.zeros((picks, reach), BF16)
        for at_col in range(0, half, TILE):
            here = parity * half + at_col
            picked = 0.0
            for lane, lines in enumerate(lanes):
                values = lines(slice(here, here + TILE))
                at = lane * lane_width(values.shape[0])
                ones = pick_ref[:, at : at + values.shape[0]]
                picked = picked + jnp.dot(ones, values, preferred_element_type=F32)
            picked = picked.astype(BF16)
            lead_ref[:, here : here + TILE] = picked[:picks]
            place = start + reach + at_col
            mate_ref[:, place : place + TILE] = picked[picks:]


def add_lines(lanes, first, are_leads, cols, pick_ref, some_leads_ref, some_mates_ref, lead_ref, mate_ref):
    half, reach = cols // 2, SPAN // 2
    padded, picks = half + 2 * reach, lead_ref.shape[0]
    to_leads = are_leads.astype(F32)
    rows = pl.ds(pl.multiple_of(jnp.where(are_leads, 0, picks), picks), picks)
    mate_ref[...] = some_mates_ref[...]
    for parity in range(2):
        for at_col in range(0, half, TILE):
            here = parity * half + at_col
            picked = 0.0
            for lane, lines in enumerate(lanes):
                values = lines(slice(here, here + TILE))
                at = (first + lane) * lane_width(values.shape[0])
                picked = picked + jnp.dot(pick_ref[rows, at : at + values.shape[0]], values, preferred_element_type=F32)
            span = slice(here, here + TILE)
            lead_ref[:, span] = (some_leads_ref[:, span].astype(F32) + picked * to_leads).astype(BF16)
            place = parity * padded + reach + at_col
            span = slice(place, place + TILE)
            mate_ref[:, span] = (some_mates_ref[:, span].astype(F32) + picked * (1.0 - to_leads)).astype(BF16)


def correlate(share, slots, cols, add, lead_ref, mate_ref, ls_ref, ms_ref):
    half, reach = cols // 2, SPAN // 2
    padded, width = half + 2 * reach, CELL + 2 * reach
    cells = half // CELL

    def one_row(row, _):
        span = pl.ds(pl.multiple_of(row * slots, slots), slots)
        for cell in range(cells):
            stack = slice(cell * slots, (cell + 1) * slots)
            back = (cells - 1 - cell) * CELL
            for parity in range(2):
                at = parity * half + cell * CELL
                ls_ref[stack, parity * CELL : (parity + 1) * CELL] = lead_ref[span, at : at + CELL]
                at = parity * padded + back
                ms_ref[stack, parity * width : (parity + 1) * width] = mate_ref[span, at : at + width]
        products = lax.dot_general(ls_ref[...], ms_ref[...], (((0,), (0,)), ((), ())), preferred_element_type=F32)
        tables = (
            products[:CELL, :width],
            products[CELL:, width:],
            products[:CELL, width:] + products[CELL:, :width],
        )
        for number, table in enumerate(tables):
            skewed = pltpu.roll(table, 0, 1, stride=1, stride_axis=0)
            add(row, number, jnp.sum(skewed, axis=0, keepdims=True))
        return 0

    lax.fori_loop(0, share, one_row, 0, unroll=UNROLL)


def select_shifts(profile_ref, shifts, scale, width):
    reach = SPAN // 2
    middle = CELL + reach - 1 - lax.shift_right_arithmetic(shifts, 1)
    odd = (shifts & 1) == 1
    wanted = (jnp.where(odd, middle, -1), jnp.where(odd, middle - 1, -1), jnp.where(odd, -1, middle))
    at = lax.broadcasted_iota(jnp.int32, (width, shifts.shape[1]), 0)
    total = jnp.zeros((profile_ref.shape[0], shifts.shape[1]), F32)
    for number, place in enumerate(wanted):
        selector = (at == place).astype(F32).astype(BF16)
        rest = profile_ref[:, number * width : (number + 1) * width]
        for _ in range(3):
            high = rest.astype(BF16)
            total = total + jnp.dot(high, selector, preferred_element_type=F32)
            rest = rest - high.astype(F32)
    return total * scale


def flat(ref, span, first=None, count=None):
    part = ref[:, :, span] if first is None else ref[first : first + count, :, span]
    return part.reshape(part.shape[0] * part.shape[1], part.shape[2])


def finish_kernel(
    upper, slot_count, ang_count, wants_inner, parts, has_out, has_old, has_other, share, slots, scale, *refs
):
    refs = list(refs)
    take = lambda count: [refs.pop(0) for _ in range(count)]
    late = ang_count - late_lanes(ang_count)
    lanes = ang_count if 1 in parts else late
    last, loads, gives_own = 1 in parts, 0 in parts, parts == (0,)
    place_ref, *ramp_refs = take(4)
    slot_refs, pieces = take(slot_count), take(lanes - 1 if loads else lanes)
    picks = dict(zip((0, 1) if loads else (1,), take(2 if loads else 1)))
    some_leads_ref, some_mates_ref = take(2) if not loads else (None, None)
    (shifts_ref,) = take(1) if last else (None,)
    take(1 if has_out else 0)
    (old_ref,) = take(1) if has_old else (None,)
    (other_ref,) = take(1) if has_other else (None,)
    out_ref, result_ref = take(2)
    own_ref, leads_out_ref, mates_out_ref = take(3) if gives_own else (None,) * 3
    (x_ref,) = take(1) if loads else (None,)
    y_ref, in_sems, out_sems, profile_ref = take(4)
    me, turn = place_ref[0], place_ref[2]
    active = place_ref[3] == wants_inner
    groups, lines_each, cols = pieces[0].shape

    @pl.when(active)
    def _():
        if loads:
            targets = [x_ref.at[:groups]] + ([own_ref] if gives_own else [])
            sems = (in_sems.at[0], in_sems.at[ang_count])
            for number, slot in enumerate(slot_refs):

                @pl.when(me ^ (turn // upper) == number)
                def _():
                    for target, sem in zip(targets, sems):
                        pltpu.make_async_copy(slot.at[:, turn % upper], target, sem).start()

            copies = [pltpu.make_async_copy(slot_refs[0].at[:, 0], target, sem) for target, sem in zip(targets, sems)]
            for lane in range(1, lanes):
                target = x_ref.at[lane * groups : (lane + 1) * groups]
                copies.append(pltpu.make_async_copy(pieces[lane - 1], target, in_sems.at[lane]))
                copies[-1].start()
            for copy in copies:
                copy.wait()
            known = [lambda span, at=lane * groups: flat(x_ref, span, at, groups) for lane in range(lanes)]
        else:
            known = [lambda span, ref=piece: flat(ref, span) for piece in pieces]
        width = CELL + SPAN
        started = []
        for number, part in enumerate(parts):
            low, high = (0 if part == 0 else late, late if parts == (0,) else ang_count)

            def lines(span, low=low, high=high):
                if loads:
                    return flat(x_ref, span, low * groups, (high - low) * groups)
                values = [read(span) for read in known[low:high]]
                return values[0] if len(values) == 1 else jnp.concatenate(values, axis=0)

            base = 0 if loads else late

            def store(block, values, low=low - base, high=high - base):
                here = slice(block * TILE, (block + 1) * TILE)
                y_ref[low * groups : high * groups, :, here] = values.reshape((high - low) * groups, lines_each, TILE)

            if number == 0:
                ramp_lines(lines, cols // 2, *ramp_refs, store)
            for lane in range(low, high) if number == 0 else ():
                target = out_ref.at[pl.ds((turn ^ lane) * groups, groups)]
                source = y_ref.at[(lane - base) * groups : (lane - base + 1) * groups]
                started.append(pltpu.make_async_copy(source, target, out_sems.at[lane]))
                started[-1].start()

            def add(row, table, values, number=number, part=part):
                at = (pl.ds(row, 1), slice(table * width, (table + 1) * width))
                if number:
                    values = values + profile_ref[at]
                elif part:
                    values = values + old_ref[at]
                profile_ref[at] = values

            lead_ref, mate_ref, *stacks = refs
            if loads:
                pick_lines(known[: late if part == 0 else ang_count], cols, picks[part], lead_ref, mate_ref)
            else:
                are_leads = (turn ^ late) < ang_count // 2
                add_lines(
                    known[late:], late, are_leads, cols, picks[1], some_leads_ref, some_mates_ref, lead_ref, mate_ref
                )
            correlate(share, slots, cols, add, lead_ref, mate_ref, *stacks)
        if gives_own:
            pick_lines(known, cols, picks[1], leads_out_ref, mates_out_ref)
        result_ref[...] = select_shifts(profile_ref, shifts_ref[...], scale, width) if last else profile_ref[...]
        for copy in started:
            copy.wait()

    @pl.when(jnp.logical_not(active))
    def _():
        result_ref[...] = other_ref[...] if has_other else jnp.zeros(result_ref.shape, F32)


def finish(place, ramp, slots, pieces, picks, some, shifts, out, old, other, wants_inner, parts, upper, share, half, after):
    loads, last, gives_own = 0 in parts, 1 in parts, parts == (0,)
    ang_count = len(pieces) + (1 if loads else 0)
    groups, lines_each, cols = pieces[0].shape
    lanes = ang_count if last else ang_count - late_lanes(ang_count)
    number = pair_slots(half)
    pieces = pieces[: lanes - 1] if loads else pieces
    args = [place, *ramp, *slots, *pieces, *(picks if loads else picks[1:]), *some]
    specs = [pl.BlockSpec(memory_space=pltpu.SMEM)] + whole(3)
    specs = specs + (anywhere if loads else whole)(len(slots) + len(pieces)) + whole(2 if loads else 1 + len(some))
    cells, width = cols // (2 * CELL), CELL + SPAN
    if last:
        args, specs = args + [shifts], specs + whole(1)
    aliases = {}
    if out is not None:
        aliases[len(args)] = 0
        args, specs = args + [out], specs + anywhere(1)
    if old is not None:
        args, specs = args + [old], specs + whole(1)
    if other is not None:
        args, specs = args + [other], specs + whole(1)
    args, specs = args + [after], specs + anywhere(1)
    kernel = functools.partial(
        finish_kernel, upper, len(slots), ang_count, wants_inner, parts, out is not None, old is not None,
        other is not None, share, number, (half * cols) ** (-0.5),
    )
    lines = lambda count: (groups * count, lines_each, cols)
    return pl.pallas_call(
        skipping(kernel, len(args) - 1),
        out_shape=[
            jax.ShapeDtypeStruct(lines(ang_count), BF16),
            jax.ShapeDtypeStruct((share, shifts.shape[1] if last else 3 * width), F32),
        ]
        + [
            jax.ShapeDtypeStruct(lines(1), BF16),
            jax.ShapeDtypeStruct((share * number, cols), BF16),
            jax.ShapeDtypeStruct((share * number, cols + 2 * SPAN), BF16),
        ]
        * gives_own,
        in_specs=specs,
        out_specs=anywhere(1) + whole(1 + 3 * gives_own),
        scratch_shapes=[pltpu.VMEM(lines(lanes), BF16)] * loads
        + [
            pltpu.VMEM(lines(lanes if loads else late_lanes(ang_count)), BF16),
            pltpu.SemaphoreType.DMA((ang_count + 1,)),
            pltpu.SemaphoreType.DMA((ang_count,)),
            pltpu.VMEM((share, 3 * width), F32),
            pltpu.VMEM((share * number, cols), BF16),
            pltpu.VMEM((share * number, cols + 2 * SPAN), BF16),
            pltpu.VMEM((cells * number, 2 * CELL), BF16),
            pltpu.VMEM((cells * number, 2 * width), BF16),
        ],
        input_output_aliases=aliases,
        compiler_params=call_params(),
        cost_estimate=cost(5.0 * len(parts)),
    )(*args)


def shards(raw_frames, dark_field, flat_field, kernel_taps, partner, shifts):
    planes, rows, cols = raw_frames.shape
    tap_count = kernel_taps.shape[0]
    half = partner.shape[0]
    row_count, ang_count = lax.axis_size("row"), lax.axis_size("ang")
    upper, share = ang_count // row_count, rows // ang_count
    me, turn = lax.axis_index("row"), lax.axis_index("ang")
    is_inner = lambda at: jnp.logical_and(at > 0, at < row_count - 1).astype(jnp.int32)
    place = jnp.stack([me, is_inner(me), turn, is_inner(turn // upper)]).astype(jnp.int32)

    cross = [(i, i + 1) for i in range(1, row_count - 1, 2)]
    near, far = edges(place, raw_frames, dark_field, flat_field)
    far = lax.ppermute(far, "row", cross + [(j, i) for i, j in cross])
    near = lax.ppermute(near, "row", [(i, i ^ 1) for i in range(row_count)])
    ext = rows + 2 * HALO
    rowband, farband, colband = pl.pallas_call(
        functools.partial(band_kernel, tap_count, rows, row_count, upper, share),
        out_shape=[
            jax.ShapeDtypeStruct((2 * GROUP * rows, GROUP * ext), BF16),
            jax.ShapeDtypeStruct((2 * GROUP * rows, GROUP * HALO), BF16),
            jax.ShapeDtypeStruct((2, TILE + 2 * CELL, TILE), BF16),
        ],
        in_specs=[pl.BlockSpec(memory_space=pltpu.SMEM)] * 2,
        out_specs=whole(3),
        compiler_params=call_params(),
        cost_estimate=cost(2.0),
    )(place, kernel_taps)
    ramp = pl.pallas_call(
        functools.partial(ramp_kernel, cols),
        out_shape=[jax.ShapeDtypeStruct((cols - TILE, TILE), BF16)] * 2 + [jax.ShapeDtypeStruct((TILE, TILE), BF16)],
        out_specs=whole(3),
        compiler_params=call_params(),
        cost_estimate=cost(1.8),
    )()

    number, late = pair_slots(half), late_lanes(ang_count)

    per_lane = lane_width(planes * share)
    picks = pl.pallas_call(
        functools.partial(pick_kernel, planes, half, number, share),
        out_shape=[
            jax.ShapeDtypeStruct((2 * share * number, lanes * per_lane), BF16) for lanes in (ang_count - late, ang_count)
        ],
        in_specs=[pl.BlockSpec(memory_space=pltpu.SMEM)] * 2,
        out_specs=whole(2),
        compiler_params=call_params(),
        cost_estimate=cost(1.5),
    )(place, partner)
    shifts = shifts[None, :]

    ends = (0, row_count - 1)
    mine = lambda inner, source: (source in ends) != bool(inner)

    free = free_steps(rows, row_count, upper, share, tap_count // 2)
    sizes = (planes, rows, cols, row_count, upper, share)
    *begun, absorbed, means = lowpass_call(
        near_kernel, free, place, [raw_frames, near, dark_field, flat_field, rowband, colband], *sizes, row_count,
        [jax.ShapeDtypeStruct((planes * ext, cols), BF16), jax.ShapeDtypeStruct((planes * ext, CELL), BF16)],
        [pltpu.VMEM((rows + HALO, cols), F32)] * 2, 6.5, [],
    )
    ended = lowpass_call(
        far_kernel, free, place, [far, absorbed, means, rowband, farband, colband], *sizes, row_count - free, [],
        [pltpu.VMEM((planes * HALO, cols), BF16), pltpu.VMEM((planes * HALO, CELL), BF16)], 3.5,
        [begun[0], ramp[0], picks[0]],
    )

    def exchange(step, sent, wanted):
        return lax.ppermute(sent, "row", [(i, i ^ step) for i in range(row_count) if wanted(i)])

    any_row = lambda source: True
    common = [begun[0] if step == 0 else exchange(step, begun[step], any_row) for step in range(free)]
    outer = common + [exchange(step, begun[step], functools.partial(mine, 0)) for step in range(free, row_count)]
    inner = common + [exchange(step, ended[step - free], functools.partial(mine, 1)) for step in range(free, row_count)]
    if not free:
        outer[0], inner[0] = begun[0], ended[0]

    def send(step, lines, wanted):
        pairs = [(i, i ^ step) for i in range(ang_count) if wanted((i ^ step) // upper)]
        return lax.ppermute(lines, "ang", pairs)

    short, long = range(1, ang_count // 2), range(max(1, ang_count // 2), ang_count)
    routed = route(place, [outer], [(step, 0) for step in long], upper, ended[0])
    outer_long = [send(step, lines, functools.partial(mine, 0)) for step, lines in zip(long, routed)]
    steps = [(step, 1) for step in long] + [(step, None) for step in short]
    routed = route(place, [outer, inner], steps, upper, ended[0])
    shared = [send(step, lines, any_row) for step, lines in zip(short, routed[len(long) :])]
    inner_long = [send(step, lines, functools.partial(mine, 1)) for step, lines in zip(long, routed)]
    outer_lines, inner_lines = shared + outer_long, shared + inner_long
    ending = functools.partial(finish, place, ramp)
    out, ends_corr = ending(
        outer, outer_lines, picks, [], shifts, None, None, None, 0, (0, 1), upper, share, half, ended[0]
    )
    out, profile, own, *some = ending(
        inner, inner_lines, picks, [], shifts, out, None, None, 1, (0,), upper, share, half, ends_corr
    )
    filtered, correlation = ending(
        [], [own, *inner_lines], picks, some, shifts, out, profile, ends_corr, 1, (1,), upper, share, half, profile
    )
    return filtered.reshape(-1, share, cols), correlation


def solution(mesh):
    in_specs = (
        P(("scan", "ang"), "row", None),
        P("row", None),
        P("row", None),
        P(),
        P("scan"),
        P(),
    )
    out_specs = (P("scan", ("ang", "row"), None), P(("scan", "ang", "row"), None))
    return jax.shard_map(shards, mesh=mesh, in_specs=in_specs, out_specs=out_specs, check_vma=False)
```
